512 devices in a mesh: section: 2 (over core), dp: 16 (over z_hi, y), vocab: 16 (over x, z_lo).
Axes of the slice: x: 4, y: 8, z: 8 (z_hi: 2, z_lo: 4; z = z_hi * 4 + z_lo), core: 2. Of those that a mesh axis runs over, the one named last changes fastest.
Arguments:
- hidden: bfloat16 [2048, 3072], P('dp', 'section'), may hold values from -2400 to 2400
- head: bfloat16 [3072, 65536], P(('section', 'dp'), 'vocab'), may hold values from -0.109375 to 0.109375
- codes: int32 [2048, 65536], P('dp', 'vocab'), may hold values from -127 to 127
- exponents: int32 [2048, 512], P('dp', 'vocab'), may hold values from -5 to -3
- loss_weight: float32 [2048], P('dp'), may hold values from 0.5 to 4
Outputs:
- kl_loss: float32 [2048], P('dp')
- hidden_grad: bfloat16 [2048, 3072], P('dp', ('section', 'vocab'))
The draws below stay inside these ranges and needn't reach their ends.
All inputs are finite; a program needn't handle non-finite values.
Results may differ from the reference program's by a relative error of at most 0.0046.
Values may be sent and summed in bfloat16 or wider, within the bound.
No kernel may reach another device: no remote copies, remote signals or barrier semaphores. Data moves between devices by JAX's collectives and lax.ppermute only.
A program may use at most 64 MiB of HBM per device.

```python
import math
from functools import partial
import jax
import jax.numpy as jnp
from jax import lax

D = 3072
V = 65536
GROUP = 128
TEMP = 2
TOK_DEV = 128
TOKENS = 2048
N_DP = 16


def draw_hidden(key, part):
    key = jax.random.fold_in(key, 7)
    base_key = jax.random.fold_in(key, 0)
    values = jnp.clip(jax.random.normal(base_key, (TOKENS, D), jnp.float32), -6.0, 6.0)
    return values.astype(jnp.bfloat16)


def place_ends(drawn, rng, least, top_value):
    spot = [jax.random.randint(jax.random.fold_in(rng, axis), (), 0, length) for axis, length in enumerate(drawn.shape)]
    widest = drawn.shape.index(max(drawn.shape))
    beside = spot[:widest] + [(spot[widest] + 1) % drawn.shape[widest]] + spot[widest + 1:]
    return drawn.at[tuple(spot)].set(least).at[tuple(beside)].set(top_value)


def block_scale(stream_key, dims, shards, low, high):
    factor_of = 1.0
    for axis_at, shards_of in shards:
        heights = jax.random.uniform(jax.random.fold_in(jax.random.fold_in(stream_key, 6), axis_at), (shards_of,), jnp.float32, low / len(shards), high / len(shards))
        factor_of = factor_of * jnp.repeat(jnp.exp(heights), dims[axis_at] // shards_of).reshape((-1,) + (1,) * (len(dims) - 1 - axis_at))
    return factor_of


def normal_values(key, dims, width, limit, shards=(), kind=jnp.bfloat16):
    entries = jax.random.normal(key, dims, jnp.float32) * width
    if len(shards) > 0:
        entries = block_scale(key, dims, shards, -0.22, 0.18) * entries
    return jnp.clip(entries, min=-limit, max=limit).astype(kind)


def setup_inputs(seed: int = 0) -> dict:
    arg_keys = jax.random.split(jax.random.key(seed), 6)
    hidden = draw_hidden(jax.random.fold_in(arg_keys[5], 71), 0)
    head = normal_values(arg_keys[1], (D, V), D ** -0.5, 0.109375, ((0, 32), (1, 16)))
    codes = place_ends(jax.random.randint(arg_keys[2], (TOKENS, V), -127, 128), jax.random.fold_in(arg_keys[2], 1), -127, 127).astype(jnp.int32)
    exponents = place_ends(jax.random.randint(arg_keys[3], (TOKENS, V // GROUP), -5, -2), jax.random.fold_in(arg_keys[3], 1), -5, (-2) - 1).astype(jnp.int32)
    loss_weight = jnp.clip(jnp.exp(math.log(4.0) - 2.0794415 * jax.random.uniform(arg_keys[4], (TOKENS,), jnp.float32) ** block_scale(arg_keys[4], (TOKENS,), ((0, 16),), -0.2, 0.2)), 0.5, 4.0)
    return dict(hidden=hidden, head=head, codes=codes, exponents=exponents, loss_weight=loss_weight)


def one_block(head, block):
    block_hidden, block_codes, block_exps, block_weight = block
    logits = jnp.dot(block_hidden, head, preferred_element_type=jnp.float32)
    row_count = block_codes.shape[0]
    scale = jnp.exp2(block_exps.astype(jnp.float32))
    teacher = (block_codes.astype(jnp.float32).reshape(row_count, V // GROUP, GROUP) * scale[:, :, None]).reshape(row_count, V)
    scaled_s = logits / TEMP
    scaled_t = teacher / TEMP
    highest = jnp.max(scaled_s, axis=1)
    s_sum = jnp.sum(jnp.exp(scaled_s - highest[:, None]), axis=1)
    t_exp = jnp.exp(scaled_t)
    t_sum = jnp.sum(t_exp, axis=1)
    cross = jnp.sum(t_exp * (scaled_t - scaled_s), axis=1)
    student_lse = highest + jnp.log(s_sum)
    teacher_lse = jnp.log(t_sum)
    kl_loss = TEMP * TEMP * (cross / t_sum - teacher_lse + student_lse)
    logit_grad = (block_weight[:, None] * TEMP * (jnp.exp(scaled_s - student_lse[:, None]) - jnp.exp(scaled_t - teacher_lse[:, None]))).astype(jnp.bfloat16)
    hidden_grad = lax.dot_general(logit_grad, head, (((1,), (1,)), ((), ())), preferred_element_type=jnp.float32)
    return kl_loss, hidden_grad.astype(jnp.bfloat16)


def reference(hidden, head, codes, exponents, loss_weight):
    blocks = (hidden.reshape(N_DP, TOK_DEV, D), codes.reshape(N_DP, TOK_DEV, V), exponents.reshape(N_DP, TOK_DEV, V // GROUP), loss_weight.reshape(N_DP, TOK_DEV))
    kl_loss, hidden_grad = lax.map(partial(one_block, head), blocks)
    return kl_loss.reshape(TOKENS), hidden_grad.reshape(TOKENS, D)
```

```python
import jax
import jax.numpy as jnp
from jax import lax
from jax.sharding import PartitionSpec as P

GROUP = 128
TEMP = 2
NY = 8
NZH = 2
NQ = 16


def flip(x, ds, dz):
    n = NZH * NY
    perm = []
    for s in range(2):
        for zh in range(NZH):
            for y in range(NY):
                perm.append((s * n + zh * NY + y, (s ^ ds) * n + (zh ^ dz) * NY + y))
    return lax.ppermute(x, ("section", "dp"), perm)


def along_y(x, step):
    perm = [(zh * NY + y, zh * NY + (y + step) % NY) for zh in range(NZH) for y in range(NY)]
    return lax.ppermute(x, "dp", perm)


def same_y(per_section):
    n = NZH * NY * NQ
    groups = []
    for y in range(NY):
        rows = [
            [s * n + (zh * NY + y) * NQ + q for zh in range(NZH) for q in range(NQ)]
            for s in range(2)
        ]
        groups += rows if per_section else [rows[0] + rows[1]]
    return groups


def exchange(x, per_section):
    return lax.all_to_all(
        x,
        ("section", "dp", "vocab"),
        split_axis=0,
        concat_axis=0,
        axis_index_groups=same_y(per_section),
        tiled=True,
    )


def teacher_half(codes, exponents):
    rows, groups = exponents.shape
    scale = jnp.exp2(exponents.astype(jnp.float32)) / TEMP
    t = codes.astype(jnp.float32).reshape(rows, groups, GROUP) * scale[:, :, None]
    return t.reshape(rows, groups * GROUP).astype(jnp.bfloat16)


def after(x, *others):
    return lax.optimization_barrier((x,) + others)[0]


def ring(block):
    half = block.shape[0] // 2
    fwd, bwd = block, block
    parts = [(0, 0, block)]
    for step in range(1, NY // 2):
        fwd, bwd = along_y(fwd, 1), along_y(bwd, -1)
        parts.append((-step, 0, fwd))
        parts.append((step, 0, bwd))
    parts.append((NY // 2, 0, along_y(fwd[:half], 1)))
    parts.append((NY // 2, half, along_y(bwd[half:], -1)))
    return parts


def on_device(hidden, head, codes, exponents, loss_weight):
    s = lax.axis_index("section")
    dp = lax.axis_index("dp")
    zh, y = dp // NY, dp % NY
    rows, cols = head.shape
    width = cols // 4
    tok = hidden.shape[0]

    def columns(x, ds, dz):
        at = ((zh ^ dz) * 2 + (s ^ ds)) * width
        return lax.dynamic_slice_in_dim(x, at, width, axis=1)

    def both(mine, other):
        return jnp.where(
            zh == 0, jnp.concatenate([mine, other]), jnp.concatenate([other, mine])
        )

    near = jnp.concatenate([columns(head, 0, 0), flip(columns(head, 1, 0), 1, 0)], axis=0)
    near_parts = ring(near)
    away = lax.dynamic_slice_in_dim(head, (zh ^ 1) * 2 * width, 2 * width, axis=1)
    came = flip(away, 0, 1)
    came_mine = lax.dynamic_slice_in_dim(came, s * width, width, axis=1)
    came_send = lax.dynamic_slice_in_dim(came, (s ^ 1) * width, width, axis=1)
    far = jnp.concatenate([came_mine, flip(came_send, 1, 0)], axis=0)
    far_parts = ring(far)

    weights = jnp.zeros((2, NZH, NY, rows, width), head.dtype)
    for dz, parts in enumerate([near_parts, far_parts]):
        for dy, at, block in parts:
            block = block.reshape(-1, 1, 1, rows, width)
            weights = lax.dynamic_update_slice(
                weights, block, (at // rows, zh ^ dz, (y + dy) % NY, 0, 0)
            )
    weights = weights.reshape(2 * NZH * NY * rows, width)

    hidden = after(hidden, near_parts[1][2])
    h_sec = both(hidden, flip(hidden, 0, 1))
    h_all = jnp.concatenate([h_sec, flip(h_sec, 1, 0)], axis=1)
    teacher = teacher_half(codes, exponents)
    t_send = after(columns(teacher, 0, 1), near_parts[3][2])
    scaled_t = both(columns(teacher, 0, 0), flip(t_send, 0, 1)).astype(jnp.float32)
    weight = both(loss_weight, flip(after(loss_weight, near_parts[3][2]), 0, 1))

    logits = jnp.dot(h_all, weights, preferred_element_type=jnp.float32)
    scaled_s = logits / TEMP
    m = jnp.max(scaled_s, axis=1)
    t_exp = jnp.exp(scaled_t)
    stats = jnp.stack(
        [
            m,
            jnp.sum(jnp.exp(scaled_s - m[:, None]), axis=1),
            jnp.sum(t_exp, axis=1),
            jnp.sum(t_exp * (scaled_t - scaled_s), axis=1),
        ]
    )
    n = 2 * NZH * NQ
    stats = exchange(jnp.broadcast_to(stats[None], (n,) + stats.shape), False)
    top = jnp.max(stats[:, 0], axis=0)
    s_sum = jnp.sum(stats[:, 1] * jnp.exp(stats[:, 0] - top), axis=0)
    t_sum = jnp.sum(stats[:, 2], axis=0)
    cross = jnp.sum(stats[:, 3], axis=0)
    student_lse = top + jnp.log(s_sum)
    teacher_lse = jnp.log(t_sum)
    kl_loss = TEMP * TEMP * (cross / t_sum - teacher_lse + student_lse)
    kl_loss = lax.dynamic_slice_in_dim(kl_loss, zh * tok, tok)

    logit_grad = (
        weight[:, None]
        * TEMP
        * (jnp.exp(scaled_s - student_lse[:, None]) - jnp.exp(scaled_t - teacher_lse[:, None]))
    ).astype(jnp.bfloat16)

    g = lax.dot_general(
        weights, logit_grad, (((1,), (1,)), ((), ())), preferred_element_type=jnp.float32
    ).reshape(2, NQ, rows, 2 * tok)
    g = g[0] + flip(g[1].astype(jnp.bfloat16), 1, 0).astype(jnp.float32)
    g = g.astype(jnp.bfloat16)
    g = jnp.concatenate([g[:, :, :tok], g[:, :, tok:]])
    g = exchange(g, True)
    g = jnp.sum(g.astype(jnp.float32), axis=0)
    return (kl_loss, g.T.astype(jnp.bfloat16))


def solution(mesh):
    in_specs = (
        P("dp", "section"),
        P(("section", "dp"), "vocab"),
        P("dp", "vocab"),
        P("dp", "vocab"),
        P("dp"),
    )
    out_specs = (P("dp"), P("dp", ("section", "vocab")))
    return jax.shard_map(
        on_device, mesh=mesh, in_specs=in_specs, out_specs=out_specs, check_vma=False
    )
```

```python
import jax
import jax.numpy as jnp
from jax import lax
from jax.sharding import PartitionSpec as P

GROUP = 128
TEMP = 2
NY = 8
NZH = 2
NQ = 16
NZL = 4


def flip(x, ds, dz):
    n = NZH * NY
    perm = []
    for s in range(2):
        for zh in range(NZH):
            for y in range(NY):
                perm.append((s * n + zh * NY + y, (s ^ ds) * n + (zh ^ dz) * NY + y))
    return lax.ppermute(x, ("section", "dp"), perm)


def along_y(x, step):
    perm = [(zh * NY + y, zh * NY + (y + step) % NY) for zh in range(NZH) for y in range(NY)]
    return lax.ppermute(x, "dp", perm)


def exchange(x):
    n = NZH * NY * NQ
    groups = [
        [s * n + (zh * NY + y) * NQ + q for zh in range(NZH) for q in range(NQ)]
        for s in range(2)
        for y in range(NY)
    ]
    return lax.all_to_all(
        x,
        ("section", "dp", "vocab"),
        split_axis=0,
        concat_axis=0,
        axis_index_groups=groups,
        tiled=True,
    )


def teacher_half(codes, exponents):
    rows, groups = exponents.shape
    scale = jnp.exp2(exponents.astype(jnp.float32)) / TEMP
    t = codes.astype(jnp.float32).reshape(rows, groups, GROUP) * scale[:, :, None]
    return t.reshape(rows, groups * GROUP).astype(jnp.bfloat16)


def along_x(x, bit):
    return lax.ppermute(x, "vocab", [(q, q ^ (bit * NZL)) for q in range(NQ)])


def after(x, *others):
    return lax.optimization_barrier((x,) + others)[0]


def reach(block, first3=(), first4=()):
    half = block.shape[0] // 2
    parts, one, two = [(0, 0, block)], {}, {}
    for way in (1, -1):
        one[way] = along_y(block, way)
        parts.append((-way, 0, one[way]))
    for way in (1, -1):
        two[way] = along_y(block, 2 * way)
        parts.append((-2 * way, 0, two[way]))
    for way in (1, -1):
        parts.append((-3 * way, 0, along_y(after(one[way], *first3), 2 * way)))
    for way, at in ((1, 0), (-1, half)):
        send = after(two[way][at : at + half], *first4)
        parts.append((NY // 2, at, along_y(send, 2 * way)))
    return parts


def on_device(hidden, head, codes, exponents, loss_weight):
    s = lax.axis_index("section")
    dp = lax.axis_index("dp")
    zh, y = dp // NY, dp % NY
    x = lax.axis_index("vocab") // NZL
    rows, cols = head.shape
    width = cols // 4
    tok, feats = hidden.shape

    def columns(a, ds, dz):
        at = ((zh ^ dz) * 2 + (s ^ ds)) * width
        return lax.dynamic_slice_in_dim(a, at, width, axis=1)

    def both(mine, other, which, axis=0):
        return jnp.where(
            which == 0,
            jnp.concatenate([mine, other], axis),
            jnp.concatenate([other, mine], axis),
        )

    near = jnp.concatenate([columns(head, 0, 0), flip(columns(head, 1, 0), 1, 0)], axis=0)
    away = lax.dynamic_slice_in_dim(head, (zh ^ 1) * 2 * width, 2 * width, axis=1)
    came = flip(away, 0, 1)
    near_parts = reach(near)
    came = after(came, near_parts[3][2], near_parts[4][2])
    came_mine = lax.dynamic_slice_in_dim(came, s * width, width, axis=1)
    came_send = lax.dynamic_slice_in_dim(came, (s ^ 1) * width, width, axis=1)
    came_flip = flip(came_send, 1, 0)

    teacher = teacher_half(codes, exponents)
    part = feats // 4
    h_send = lax.dynamic_slice_in_dim(hidden, x * part, part, axis=1)
    sent = jnp.concatenate([columns(teacher, 0, 1), h_send], axis=1)
    got = flip(after(sent, came_flip), 0, 1)
    far_parts = reach(jnp.concatenate([came_mine, came_flip], axis=0), (got,))
    scaled_t = both(columns(teacher, 0, 0), got[:, :width], zh).astype(jnp.float32)

    weights = jnp.zeros((2, NZH, NY, rows, width), head.dtype)
    for dz, parts in enumerate([near_parts, far_parts]):
        for dy, at, block in parts:
            block = block.reshape(-1, 1, 1, rows, width)
            weights = lax.dynamic_update_slice(
                weights, block, (at // rows, zh ^ dz, (y + dy) % NY, 0, 0)
            )
    weights = weights.reshape(2 * NZH * NY * rows, width)

    h_other = after(got, *[block for _, _, block in far_parts[1:5]])[:, width:]
    h_other = both(h_other, along_x(h_other, 1), x % 2, axis=1)
    h_other = both(h_other, along_x(h_other, 2), x // 2, axis=1)
    h_sec = both(hidden, h_other, zh)
    h_all = jnp.concatenate([h_sec, flip(h_sec, 1, 0)], axis=1)

    logits = jnp.dot(h_all, weights, preferred_element_type=jnp.float32)
    scaled_s = logits / TEMP
    m = jnp.max(scaled_s, axis=1)
    t_exp = jnp.exp(scaled_t)
    stats = jnp.stack(
        [
            m,
            jnp.sum(jnp.exp(scaled_s - m[:, None]), axis=1),
            jnp.sum(t_exp, axis=1),
            jnp.sum(t_exp * (scaled_t - scaled_s), axis=1),
        ]
    ).reshape(8, tok)

    stats = jnp.stack([stats, flip(stats, 1, 0)])
    top = jnp.max(stats[:, 0:2], axis=0)
    s_sum = jnp.sum(stats[:, 2:4] * jnp.exp(stats[:, 0:2] - top), axis=0)
    rest = jnp.sum(stats[:, 4:8], axis=0)
    tiles = [
        jnp.concatenate([top, s_sum, rest[0:2], rest[2 + z : 3 + z], loss_weight[None]])
        for z in range(NZH)
    ]
    parts = jnp.broadcast_to(jnp.stack(tiles)[:, None], (NZH, NQ, 8, tok))
    parts = exchange(parts.reshape(NZH * NQ, 8, tok))
    top = jnp.max(parts[:, 0:2], axis=0)
    s_sum = jnp.sum(parts[:, 2:4] * jnp.exp(parts[:, 0:2] - top), axis=0)
    t_sum = jnp.sum(parts[:, 4:6], axis=0)
    cross = jnp.sum(parts[:, 6], axis=0)
    weight = jnp.concatenate([parts[0, 7], parts[NQ, 7]])
    student_lse = top + jnp.log(s_sum)
    teacher_lse = jnp.log(t_sum)

    def of_mine(a):
        return lax.dynamic_index_in_dim(a, zh, axis=0, keepdims=False)

    kl_loss = cross / of_mine(t_sum) - of_mine(teacher_lse) + of_mine(student_lse)
    kl_loss = TEMP * TEMP * kl_loss

    student_lse, teacher_lse = student_lse.reshape(2 * tok), teacher_lse.reshape(2 * tok)
    logit_grad = (
        weight[:, None]
        * TEMP
        * (jnp.exp(scaled_s - student_lse[:, None]) - jnp.exp(scaled_t - teacher_lse[:, None]))
    ).astype(jnp.bfloat16)

    g = lax.dot_general(
        weights, logit_grad, (((1,), (1,)), ((), ())), preferred_element_type=jnp.float32
    ).reshape(2, NQ, rows, 2 * tok)
    g = g[0] + flip(g[1].astype(jnp.bfloat16), 1, 0).astype(jnp.float32)
    g = g.astype(jnp.bfloat16).reshape(NQ, rows, 2, tok)
    g = g.transpose(2, 0, 1, 3).reshape(NZH * NQ, rows, tok)
    g = exchange(g)
    g = jnp.sum(g.astype(jnp.float32), axis=0)
    return (kl_loss, g.T.astype(jnp.bfloat16))


def solution(mesh):
    in_specs = (
        P("dp", "section"),
        P(("section", "dp"), "vocab"),
        P("dp", "vocab"),
        P("dp", "vocab"),
        P("dp"),
    )
    out_specs = (P("dp"), P("dp", ("section", "vocab")))
    return jax.shard_map(
        on_device, mesh=mesh, in_specs=in_specs, out_specs=out_specs, check_vma=False
    )
```

```python
import jax
import jax.numpy as jnp
from jax import lax
from jax.sharding import PartitionSpec as P

GROUP = 128
TEMP = 2
NY = 8
NZH = 2
NQ = 16


def flip(x, ds, dz):
    n = NZH * NY
    perm = []
    for s in range(2):
        for zh in range(NZH):
            for y in range(NY):
                perm.append((s * n + zh * NY + y, (s ^ ds) * n + (zh ^ dz) * NY + y))
    return lax.ppermute(x, ("section", "dp"), perm)


def along_y(x, step):
    perm = [(zh * NY + y, zh * NY + (y + step) % NY) for zh in range(NZH) for y in range(NY)]
    return lax.ppermute(x, "dp", perm)


def exchange(x):
    n = NZH * NY * NQ
    groups = [
        [s * n + (zh * NY + y) * NQ + q for zh in range(NZH) for q in range(NQ)]
        for s in range(2)
        for y in range(NY)
    ]
    return lax.all_to_all(
        x,
        ("section", "dp", "vocab"),
        split_axis=0,
        concat_axis=0,
        axis_index_groups=groups,
        tiled=True,
    )


def teacher_half(codes, exponents):
    rows, groups = exponents.shape
    scale = jnp.exp2(exponents.astype(jnp.float32)) / TEMP
    t = codes.astype(jnp.float32).reshape(rows, groups, GROUP) * scale[:, :, None]
    return t.reshape(rows, groups * GROUP).astype(jnp.bfloat16)


def after(x, *others):
    return lax.optimization_barrier((x,) + others)[0]


def ring(block):
    half = block.shape[0] // 2
    fwd, bwd = block, block
    parts = [(0, 0, block)]
    for step in range(1, NY // 2):
        fwd, bwd = along_y(fwd, 1), along_y(bwd, -1)
        parts.append((-step, 0, fwd))
        parts.append((step, 0, bwd))
    parts.append((NY // 2, 0, along_y(fwd[:half], 1)))
    parts.append((NY // 2, half, along_y(bwd[half:], -1)))
    return parts


def on_device(hidden, head, codes, exponents, loss_weight):
    s = lax.axis_index("section")
    dp = lax.axis_index("dp")
    zh, y = dp // NY, dp % NY
    rows, cols = head.shape
    width = cols // 4
    tok = hidden.shape[0]

    def columns(x, ds, dz):
        at = ((zh ^ dz) * 2 + (s ^ ds)) * width
        return lax.dynamic_slice_in_dim(x, at, width, axis=1)

    def both(mine, other):
        return jnp.where(
            zh == 0, jnp.concatenate([mine, other]), jnp.concatenate([other, mine])
        )

    near = jnp.concatenate([columns(head, 0, 0), flip(columns(head, 1, 0), 1, 0)], axis=0)
    near_parts = ring(near)
    away = lax.dynamic_slice_in_dim(head, (zh ^ 1) * 2 * width, 2 * width, axis=1)
    came = flip(away, 0, 1)
    came_mine = lax.dynamic_slice_in_dim(came, s * width, width, axis=1)
    came_send = lax.dynamic_slice_in_dim(came, (s ^ 1) * width, width, axis=1)
    far = jnp.concatenate([came_mine, flip(came_send, 1, 0)], axis=0)
    far_parts = ring(far)

    weights = jnp.zeros((2, NZH, NY, rows, width), head.dtype)
    for dz, parts in enumerate([near_parts, far_parts]):
        for dy, at, block in parts:
            block = block.reshape(-1, 1, 1, rows, width)
            weights = lax.dynamic_update_slice(
                weights, block, (at // rows, zh ^ dz, (y + dy) % NY, 0, 0)
            )
    weights = weights.reshape(2 * NZH * NY * rows, width)

    hidden = after(hidden, near_parts[1][2])
    h_sec = both(hidden, flip(hidden, 0, 1))
    h_all = jnp.concatenate([h_sec, flip(h_sec, 1, 0)], axis=1)
    teacher = teacher_half(codes, exponents)
    t_send = after(columns(teacher, 0, 1), near_parts[3][2])
    scaled_t = both(columns(teacher, 0, 0), flip(t_send, 0, 1)).astype(jnp.float32)

    logits = jnp.dot(h_all, weights, preferred_element_type=jnp.float32)
    scaled_s = logits / TEMP
    m = jnp.max(scaled_s, axis=1)
    t_exp = jnp.exp(scaled_t)
    stats = jnp.stack(
        [
            m,
            jnp.sum(jnp.exp(scaled_s - m[:, None]), axis=1),
            jnp.sum(t_exp, axis=1),
            jnp.sum(t_exp * (scaled_t - scaled_s), axis=1),
        ]
    ).reshape(8, tok)

    stats = jnp.stack([stats, flip(stats, 1, 0)])
    top = jnp.max(stats[:, 0:2], axis=0)
    s_sum = jnp.sum(stats[:, 2:4] * jnp.exp(stats[:, 0:2] - top), axis=0)
    rest = jnp.sum(stats[:, 4:8], axis=0)
    tiles = [
        jnp.concatenate([top, s_sum, rest[0:2], rest[2 + z : 3 + z], loss_weight[None]])
        for z in range(NZH)
    ]
    parts = jnp.broadcast_to(jnp.stack(tiles)[:, None], (NZH, NQ, 8, tok))
    parts = exchange(parts.reshape(NZH * NQ, 8, tok))
    top = jnp.max(parts[:, 0:2], axis=0)
    s_sum = jnp.sum(parts[:, 2:4] * jnp.exp(parts[:, 0:2] - top), axis=0)
    t_sum = jnp.sum(parts[:, 4:6], axis=0)
    cross = jnp.sum(parts[:, 6], axis=0)
    weight = jnp.concatenate([parts[0, 7], parts[NQ, 7]])
    student_lse = top + jnp.log(s_sum)
    teacher_lse = jnp.log(t_sum)

    def of_mine(a):
        return lax.dynamic_index_in_dim(a, zh, axis=0, keepdims=False)

    kl_loss = cross / of_mine(t_sum) - of_mine(teacher_lse) + of_mine(student_lse)
    kl_loss = TEMP * TEMP * kl_loss

    student_lse, teacher_lse = student_lse.reshape(2 * tok), teacher_lse.reshape(2 * tok)
    logit_grad = (
        weight[:, None]
        * TEMP
        * (jnp.exp(scaled_s - student_lse[:, None]) - jnp.exp(scaled_t - teacher_lse[:, None]))
    ).astype(jnp.bfloat16)

    g = lax.dot_general(
        weights, logit_grad, (((1,), (1,)), ((), ())), preferred_element_type=jnp.float32
    ).reshape(2, NQ, rows, 2 * tok)
    g = g[0] + flip(g[1].astype(jnp.bfloat16), 1, 0).astype(jnp.float32)
    g = g.astype(jnp.bfloat16).reshape(NQ, rows, 2, tok)
    g = g.transpose(2, 0, 1, 3).reshape(NZH * NQ, rows, tok)
    g = exchange(g)
    g = jnp.sum(g.astype(jnp.float32), axis=0)
    return (kl_loss, g.T.astype(jnp.bfloat16))


def solution(mesh):
    in_specs = (
        P("dp", "section"),
        P(("section", "dp"), "vocab"),
        P("dp", "vocab"),
        P("dp", "vocab"),
        P("dp"),
    )
    out_specs = (P("dp"), P("dp", ("section", "vocab")))
    return jax.shard_map(
        on_device, mesh=mesh, in_specs=in_specs, out_specs=out_specs, check_vma=False
    )
```

```python
import jax
import jax.numpy as jnp
from jax import lax
from jax.sharding import PartitionSpec as P

GROUP = 128
TEMP = 2
NY = 8
NZH = 2
NQ = 16


def flip(x, ds, dz):
    n = NZH * NY
    perm = []
    for s in range(2):
        for zh in range(NZH):
            for y in range(NY):
                perm.append((s * n + zh * NY + y, (s ^ ds) * n + (zh ^ dz) * NY + y))
    return lax.ppermute(x, ("section", "dp"), perm)


def along_y(x, step):
    perm = [(zh * NY + y, zh * NY + (y + step) % NY) for zh in range(NZH) for y in range(NY)]
    return lax.ppermute(x, "dp", perm)


def exchange(x):
    n = NZH * NY * NQ
    groups = [
        [s * n + (zh * NY + y) * NQ + q for zh in range(NZH) for q in range(NQ)]
        for s in range(2)
        for y in range(NY)
    ]
    return lax.all_to_all(
        x,
        ("section", "dp", "vocab"),
        split_axis=0,
        concat_axis=0,
        axis_index_groups=groups,
        tiled=True,
    )


def teacher_half(codes, exponents):
    rows, groups = exponents.shape
    scale = jnp.exp2(exponents.astype(jnp.float32)) / TEMP
    t = codes.astype(jnp.float32).reshape(rows, groups, GROUP) * scale[:, :, None]
    return t.reshape(rows, groups * GROUP).astype(jnp.bfloat16)


def after(x, *others):
    return lax.optimization_barrier((x,) + others)[0]


def rings(blocks):
    half = blocks[0].shape[0] // 2
    all_parts, ends = [], {1: [], -1: []}
    for block in blocks:
        fwd, bwd = block, block
        parts = [(0, 0, block)]
        for step in range(1, NY // 2):
            fwd, bwd = along_y(fwd, 1), along_y(bwd, -1)
            parts.append((-step, 0, fwd))
            parts.append((step, 0, bwd))
        ends[1].append(fwd[:half])
        ends[-1].append(bwd[half:])
        all_parts.append(parts)
    for way, at in ((1, 0), (-1, half)):
        last = along_y(jnp.concatenate(ends[way]), way)
        for parts, block in zip(all_parts, jnp.split(last, len(blocks))):
            parts.append((NY // 2, at, block))
    return all_parts


def on_device(hidden, head, codes, exponents, loss_weight):
    s = lax.axis_index("section")
    dp = lax.axis_index("dp")
    zh, y = dp // NY, dp % NY
    rows, cols = head.shape
    width = cols // 4
    tok = hidden.shape[0]

    def columns(x, ds, dz):
        at = ((zh ^ dz) * 2 + (s ^ ds)) * width
        return lax.dynamic_slice_in_dim(x, at, width, axis=1)

    def both(mine, other):
        return jnp.where(
            zh == 0, jnp.concatenate([mine, other]), jnp.concatenate([other, mine])
        )

    near = jnp.concatenate([columns(head, 0, 0), flip(columns(head, 1, 0), 1, 0)], axis=0)
    away = lax.dynamic_slice_in_dim(head, (zh ^ 1) * 2 * width, 2 * width, axis=1)
    came = flip(away, 0, 1)
    teacher = teacher_half(codes, exponents)
    came = after(came, along_y(near, 1), along_y(near, -1), teacher)
    came_mine = lax.dynamic_slice_in_dim(came, s * width, width, axis=1)
    came_send = lax.dynamic_slice_in_dim(came, (s ^ 1) * width, width, axis=1)
    far = jnp.concatenate([came_mine, flip(came_send, 1, 0)], axis=0)
    near_parts, far_parts = rings([near, far])

    weights = jnp.zeros((2, NZH, NY, rows, width), head.dtype)
    for dz, parts in enumerate([near_parts, far_parts]):
        for dy, at, block in parts:
            block = block.reshape(-1, 1, 1, rows, width)
            weights = lax.dynamic_update_slice(
                weights, block, (at // rows, zh ^ dz, (y + dy) % NY, 0, 0)
            )
    weights = weights.reshape(2 * NZH * NY * rows, width)

    hidden = after(hidden, near_parts[1][2])
    h_sec = both(hidden, flip(hidden, 0, 1))
    h_all = jnp.concatenate([h_sec, flip(h_sec, 1, 0)], axis=1)
    t_send = after(columns(teacher, 0, 1), near_parts[3][2])
    scaled_t = both(columns(teacher, 0, 0), flip(t_send, 0, 1)).astype(jnp.float32)

    logits = jnp.dot(h_all, weights, preferred_element_type=jnp.float32)
    scaled_s = logits / TEMP
    m = jnp.max(scaled_s, axis=1)
    t_exp = jnp.exp(scaled_t)
    stats = jnp.stack(
        [
            m,
            jnp.sum(jnp.exp(scaled_s - m[:, None]), axis=1),
            jnp.sum(t_exp, axis=1),
            jnp.sum(t_exp * (scaled_t - scaled_s), axis=1),
        ]
    ).reshape(8, tok)

    stats = jnp.stack([stats, flip(stats, 1, 0)])
    top = jnp.max(stats[:, 0:2], axis=0)
    s_sum = jnp.sum(stats[:, 2:4] * jnp.exp(stats[:, 0:2] - top), axis=0)
    rest = jnp.sum(stats[:, 4:8], axis=0)
    tiles = [
        jnp.concatenate([top, s_sum, rest[0:2], rest[2 + z : 3 + z], loss_weight[None]])
        for z in range(NZH)
    ]
    parts = jnp.broadcast_to(jnp.stack(tiles)[:, None], (NZH, NQ, 8, tok))
    parts = exchange(parts.reshape(NZH * NQ, 8, tok))
    top = jnp.max(parts[:, 0:2], axis=0)
    s_sum = jnp.sum(parts[:, 2:4] * jnp.exp(parts[:, 0:2] - top), axis=0)
    t_sum = jnp.sum(parts[:, 4:6], axis=0)
    cross = jnp.sum(parts[:, 6], axis=0)
    weight = jnp.concatenate([parts[0, 7], parts[NQ, 7]])
    student_lse = top + jnp.log(s_sum)
    teacher_lse = jnp.log(t_sum)

    def of_mine(a):
        return lax.dynamic_index_in_dim(a, zh, axis=0, keepdims=False)

    kl_loss = cross / of_mine(t_sum) - of_mine(teacher_lse) + of_mine(student_lse)
    kl_loss = TEMP * TEMP * kl_loss

    student_lse, teacher_lse = student_lse.reshape(2 * tok), teacher_lse.reshape(2 * tok)
    logit_grad = (
        weight[:, None]
        * TEMP
        * (jnp.exp(scaled_s - student_lse[:, None]) - jnp.exp(scaled_t - teacher_lse[:, None]))
    ).astype(jnp.bfloat16)

    logit_grad = after(logit_grad)

    def grads(w):
        return lax.dot_general(
            w, logit_grad, (((1,), (1,)), ((), ())), preferred_element_type=jnp.float32
        )

    mine, theirs = jnp.split(weights, 2)
    g = flip(grads(theirs).astype(jnp.bfloat16), 1, 0).astype(jnp.float32)
    g = grads(mine) + g
    g = g.astype(jnp.bfloat16).reshape(NQ, rows, 2, tok)
    g = g.transpose(2, 0, 1, 3).reshape(NZH * NQ, rows, tok)
    g = exchange(g)
    g = jnp.sum(g.astype(jnp.float32), axis=0)
    return (kl_loss, g.T.astype(jnp.bfloat16))


def solution(mesh):
    in_specs = (
        P("dp", "section"),
        P(("section", "dp"), "vocab"),
        P("dp", "vocab"),
        P("dp", "vocab"),
        P("dp"),
    )
    out_specs = (P("dp"), P("dp", ("section", "vocab")))
    return jax.shard_map(
        on_device, mesh=mesh, in_specs=in_specs, out_specs=out_specs, check_vma=False
    )
```

```python
import jax
import jax.numpy as jnp
from jax import lax
from jax.experimental import pallas as pl
from jax.experimental.pallas import tpu as pltpu
from jax.sharding import PartitionSpec as P

GROUP = 128
TEMP = 2
NY = 8
NZH = 2
NQ = 16
NX = 4
NZL = 4


def flip(x, ds, dz):
    n = NZH * NY
    perm = []
    for s in range(2):
        for zh in range(NZH):
            for y in range(NY):
                perm.append((s * n + zh * NY + y, (s ^ ds) * n + (zh ^ dz) * NY + y))
    return lax.ppermute(x, ("section", "dp"), perm)


def along_y(x, step):
    perm = [(zh * NY + y, zh * NY + (y + step) % NY) for zh in range(NZH) for y in range(NY)]
    return lax.ppermute(x, "dp", perm)


def exchange(x, axis):
    n = NZH * NY * NQ

    def device(s, y, zh, x, zl):
        return s * n + (zh * NY + y) * NQ + x * NZL + zl

    rest = [(s, y) for s in range(2) for y in range(NY)]
    if axis == "x":
        groups = [
            [device(s, y, zh, x, zl) for x in range(NX)]
            for s, y in rest
            for zh in range(NZH)
            for zl in range(NZL)
        ]
    elif axis == "z":
        groups = [
            [device(s, y, zh, x, zl) for zh in range(NZH) for zl in range(NZL)]
            for s, y in rest
            for x in range(NX)
        ]
    else:
        groups = [
            [device(s, y, zh, x, zl) for zh in range(NZH) for x in range(NX) for zl in range(NZL)]
            for s, y in rest
        ]
    return lax.all_to_all(
        x,
        ("section", "dp", "vocab"),
        split_axis=0,
        concat_axis=0,
        axis_index_groups=groups,
        tiled=True,
    )


def teacher_half(codes, exponents):
    rows, groups = exponents.shape
    scale = jnp.exp2(exponents.astype(jnp.float32)) / TEMP
    t = codes.astype(jnp.float32).reshape(rows, groups, GROUP) * scale[:, :, None]
    return t.reshape(rows, groups * GROUP).astype(jnp.bfloat16)


def after(x, *others):
    return lax.optimization_barrier((x,) + others)[0]


def ring_step(parts, *others):
    block = parts[0][2]
    half = block.shape[0] // 2
    k = len(parts) // 2 + 1
    fwd, bwd = (block, block) if k == 1 else (parts[-2][2], parts[-1][2])
    if k == NY // 2:
        fwd, bwd = fwd[:half], bwd[half:]
    fwd = along_y(after(fwd, *others) if others else fwd, 1)
    bwd = along_y(after(bwd, *others) if others else bwd, -1)
    return parts + [(-k, 0, fwd), (k, half if k == NY // 2 else 0, bwd)]


def came_in(parts):
    return parts[-2][2], parts[-1][2]


def split_columns(x, s):
    rows, cols = x.shape
    half = cols // 2

    def kernel(s_ref, x_ref, mine_ref, send_ref):
        at = s_ref[0] * half
        mine_ref[...] = x_ref[:, pl.ds(pl.multiple_of(at, half), half)]
        send_ref[...] = x_ref[:, pl.ds(pl.multiple_of(half - at, half), half)]

    return pl.pallas_call(
        kernel,
        in_specs=[
            pl.BlockSpec(memory_space=pltpu.SMEM),
            pl.BlockSpec(memory_space=pltpu.VMEM),
        ],
        out_specs=[pl.BlockSpec(memory_space=pltpu.VMEM)] * 2,
        out_shape=[jax.ShapeDtypeStruct((rows, half), x.dtype)] * 2,
        cost_estimate=pl.CostEstimate(flops=10000000000, bytes_accessed=1000000, transcendentals=0),
    )(s[None], x)


def on_device(hidden, head, codes, exponents, loss_weight):
    s = lax.axis_index("section")
    dp = lax.axis_index("dp")
    zh, y = dp // NY, dp % NY
    rows, cols = head.shape
    width = cols // 4
    tok = hidden.shape[0]

    def columns(x, ds, dz):
        at = ((zh ^ dz) * 2 + (s ^ ds)) * width
        return lax.dynamic_slice_in_dim(x, at, width, axis=1)

    def both(mine, other):
        return jnp.where(
            zh == 0, jnp.concatenate([mine, other]), jnp.concatenate([other, mine])
        )

    near = jnp.concatenate([columns(head, 0, 0), flip(columns(head, 1, 0), 1, 0)], axis=0)
    away = lax.dynamic_slice_in_dim(head, (zh ^ 1) * 2 * width, 2 * width, axis=1)
    came = flip(away, 0, 1)
    teacher = teacher_half(codes, exponents)
    near_one = ring_step([(0, 0, near)])
    near_two = ring_step(near_one)
    came_mine, came_send = split_columns(came, s)
    came_mine = after(came_mine, *came_in(near_two))
    came_flip = flip(came_send, 1, 0)
    far = jnp.concatenate([came_mine, came_flip], axis=0)
    far_one = ring_step([(0, 0, far)])
    near_three = ring_step(near_two)
    far_two = ring_step(far_one, *came_in(near_three))
    far_three = ring_step(far_two)
    near_parts = ring_step(near_three)
    far_parts = ring_step(far_three)

    weights = jnp.zeros((2, NZH, NY, rows, width), head.dtype)
    for dz, parts in enumerate([near_parts, far_parts]):
        for dy, at, block in parts:
            block = block.reshape(-1, 1, 1, rows, width)
            weights = lax.dynamic_update_slice(
                weights, block, (at // rows, zh ^ dz, (y + dy) % NY, 0, 0)
            )
    weights = weights.reshape(2 * NZH * NY * rows, width)

    h_other = flip(after(hidden, came_flip), 0, 1)
    h_sec = both(hidden, after(h_other, *came_in(far_two)))
    h_all = jnp.concatenate([h_sec, flip(h_sec, 1, 0)], axis=1)
    t_send = after(columns(teacher, 0, 1), *came_in(far_one))
    scaled_t = both(columns(teacher, 0, 0), flip(t_send, 0, 1)).astype(jnp.float32)

    logits = jnp.dot(h_all, weights, preferred_element_type=jnp.float32)
    scaled_s = logits / TEMP
    m = jnp.max(scaled_s, axis=1)
    t_exp = jnp.exp(scaled_t)
    stats = jnp.stack(
        [
            m,
            jnp.sum(jnp.exp(scaled_s - m[:, None]), axis=1),
            jnp.sum(t_exp, axis=1),
            jnp.sum(t_exp * (scaled_t - scaled_s), axis=1),
        ]
    ).reshape(8, tok)

    def merged(parts):
        top = jnp.max(parts[:, 0:2], axis=0)
        s_sum = jnp.sum(parts[:, 2:4] * jnp.exp(parts[:, 0:2] - top), axis=0)
        return top, s_sum, jnp.sum(parts[:, 4:8], axis=0)

    stats = jnp.concatenate(merged(jnp.stack([stats, flip(stats, 1, 0)])))
    top, s_sum, rest = merged(exchange(jnp.broadcast_to(stats, (NX, 8, tok)), "x"))
    tiles = [
        jnp.concatenate([top, s_sum, rest[0:2], rest[2 + z : 3 + z], loss_weight[None]])
        for z in range(NZH)
    ]
    parts = jnp.broadcast_to(jnp.stack(tiles)[:, None], (NZH, NZL, 8, tok))
    parts = exchange(parts.reshape(NZH * NZL, 8, tok), "z")
    top = jnp.max(parts[:, 0:2], axis=0)
    s_sum = jnp.sum(parts[:, 2:4] * jnp.exp(parts[:, 0:2] - top), axis=0)
    t_sum = jnp.sum(parts[:, 4:6], axis=0)
    cross = jnp.sum(parts[:, 6], axis=0)
    weight = jnp.concatenate([parts[0, 7], parts[NZL, 7]])
    student_lse = top + jnp.log(s_sum)
    teacher_lse = jnp.log(t_sum)

    def of_mine(a):
        return lax.dynamic_index_in_dim(a, zh, axis=0, keepdims=False)

    kl_loss = cross / of_mine(t_sum) - of_mine(teacher_lse) + of_mine(student_lse)
    kl_loss = TEMP * TEMP * kl_loss

    student_lse, teacher_lse = student_lse.reshape(2 * tok), teacher_lse.reshape(2 * tok)
    logit_grad = (
        weight[:, None]
        * TEMP
        * (jnp.exp(scaled_s - student_lse[:, None]) - jnp.exp(scaled_t - teacher_lse[:, None]))
    ).astype(jnp.bfloat16)

    g = lax.dot_general(
        weights, logit_grad, (((1,), (1,)), ((), ())), preferred_element_type=jnp.float32
    ).reshape(2, NQ, rows, 2 * tok)
    g = g[0] + flip(g[1].astype(jnp.bfloat16), 1, 0).astype(jnp.float32)
    g = g.astype(jnp.bfloat16).reshape(NX, NZL * rows, 2 * tok)
    g = jnp.sum(exchange(g, "x").reshape(g.shape).astype(jnp.float32), axis=0)
    g = g.astype(jnp.bfloat16).reshape(NZL, rows, NZH, tok)
    g = exchange(g.transpose(2, 0, 1, 3).reshape(NZH * NZL, rows, tok), "z")
    g = jnp.sum(g.astype(jnp.float32), axis=0)
    return (kl_loss, g.T.astype(jnp.bfloat16))


def solution(mesh):
    in_specs = (
        P("dp", "section"),
        P(("section", "dp"), "vocab"),
        P("dp", "vocab"),
        P("dp", "vocab"),
        P("dp"),
    )
    out_specs = (P("dp"), P("dp", ("section", "vocab")))
    return jax.shard_map(
        on_device, mesh=mesh, in_specs=in_specs, out_specs=out_specs, check_vma=False
    )
```

```python
import jax
import jax.numpy as jnp
from jax import lax
from jax.experimental import pallas as pl
from jax.experimental.pallas import tpu as pltpu
from jax.sharding import PartitionSpec as P

GROUP = 128
TEMP = 2
NY = 8
NZH = 2
NQ = 16


def flip(x, ds, dz):
    n = NZH * NY
    perm = []
    for s in range(2):
        for zh in range(NZH):
            for y in range(NY):
                perm.append((s * n + zh * NY + y, (s ^ ds) * n + (zh ^ dz) * NY + y))
    return lax.ppermute(x, ("section", "dp"), perm)


def along_y(x, step):
    perm = [(zh * NY + y, zh * NY + (y + step) % NY) for zh in range(NZH) for y in range(NY)]
    return lax.ppermute(x, "dp", perm)


def exchange(x):
    n = NZH * NY * NQ
    groups = [
        [s * n + (zh * NY + y) * NQ + q for zh in range(NZH) for q in range(NQ)]
        for s in range(2)
        for y in range(NY)
    ]
    return lax.all_to_all(
        x,
        ("section", "dp", "vocab"),
        split_axis=0,
        concat_axis=0,
        axis_index_groups=groups,
        tiled=True,
    )


def teacher_half(codes, exponents):
    rows, groups = exponents.shape
    scale = jnp.exp2(exponents.astype(jnp.float32)) / TEMP
    t = codes.astype(jnp.float32).reshape(rows, groups, GROUP) * scale[:, :, None]
    return t.reshape(rows, groups * GROUP).astype(jnp.bfloat16)


def after(x, *others):
    return lax.optimization_barrier((x,) + others)[0]


def ring(block):
    half = block.shape[0] // 2
    fwd, bwd = block, block
    parts = [(0, 0, block)]
    for step in range(1, NY // 2):
        fwd, bwd = along_y(fwd, 1), along_y(bwd, -1)
        parts.append((-step, 0, fwd))
        parts.append((step, 0, bwd))
    parts.append((NY // 2, 0, along_y(fwd[:half], 1)))
    parts.append((NY // 2, half, along_y(bwd[half:], -1)))
    return parts


TILE = 256


def grad_rows(w_ref, section, at, logit_grad):
    rows = w_ref[section, pl.ds(pl.multiple_of(at, TILE), TILE), :]
    return lax.dot_general(
        rows, logit_grad, (((1,), (1,)), ((), ())), preferred_element_type=jnp.float32
    )


def first_grads_kernel(s_ref, t_ref, row_ref, w_ref, lg_ref, g_ref):
    student_lse, teacher_lse, weight = row_ref[:, 0:1], row_ref[:, 1:2], row_ref[:, 2:3]
    student = jnp.exp(s_ref[...] - student_lse)
    teacher = jnp.exp(t_ref[...].astype(jnp.float32) - teacher_lse)
    lg_ref[...] = (weight * TEMP * (student - teacher)).astype(jnp.bfloat16)
    logit_grad = lg_ref[...]
    tok = g_ref.shape[2]

    def step(k, carry):
        g = grad_rows(w_ref, 1, k * TILE, logit_grad).astype(jnp.bfloat16)
        for z in range(NZH):
            g_ref[z, pl.ds(pl.multiple_of(k * TILE, TILE), TILE), :] = g[:, z * tok : (z + 1) * tok]
        return carry

    lax.fori_loop(0, g_ref.shape[1] // TILE, step, 0)


def second_grads_kernel(lg_ref, w_ref, g_ref):
    logit_grad = lg_ref[...]
    tok = g_ref.shape[2]

    def step(k, carry):
        g = grad_rows(w_ref, 0, k * TILE, logit_grad)
        for z in range(NZH):
            g_ref[z, pl.ds(pl.multiple_of(k * TILE, TILE), TILE), :] = g[:, z * tok : (z + 1) * tok]
        return carry

    lax.fori_loop(0, g_ref.shape[1] // TILE, step, 0)


def in_vmem(kernel, ins, outs):
    whole = pl.BlockSpec(memory_space=pltpu.VMEM)
    return pl.pallas_call(
        kernel,
        in_specs=[whole] * len(ins),
        out_specs=[whole] * len(outs),
        out_shape=outs,
        compiler_params=pltpu.CompilerParams(vmem_limit_bytes=40 * 2**20),
        cost_estimate=pl.CostEstimate(
            flops=10**9, bytes_accessed=5 * 10**6, transcendentals=5 * 10**5
        ),
    )(*ins)


def on_device(hidden, head, codes, exponents, loss_weight):
    s = lax.axis_index("section")
    dp = lax.axis_index("dp")
    zh, y = dp // NY, dp % NY
    rows, cols = head.shape
    width = cols // 4
    tok = hidden.shape[0]

    def columns(x, ds, dz):
        at = ((zh ^ dz) * 2 + (s ^ ds)) * width
        return lax.dynamic_slice_in_dim(x, at, width, axis=1)

    def both(mine, other):
        return jnp.where(
            zh == 0, jnp.concatenate([mine, other]), jnp.concatenate([other, mine])
        )

    near = jnp.concatenate([columns(head, 0, 0), flip(columns(head, 1, 0), 1, 0)], axis=0)
    near_parts = ring(near)
    away = lax.dynamic_slice_in_dim(head, (zh ^ 1) * 2 * width, 2 * width, axis=1)
    came = flip(away, 0, 1)
    came_mine = lax.dynamic_slice_in_dim(came, s * width, width, axis=1)
    came_send = lax.dynamic_slice_in_dim(came, (s ^ 1) * width, width, axis=1)
    far = jnp.concatenate([came_mine, flip(came_send, 1, 0)], axis=0)
    far_parts = ring(far)

    weights = jnp.zeros((2, NZH, NY, rows, width), head.dtype)
    for dz, parts in enumerate([near_parts, far_parts]):
        for dy, at, block in parts:
            block = block.reshape(-1, 1, 1, rows, width)
            weights = lax.dynamic_update_slice(
                weights, block, (at // rows, zh ^ dz, (y + dy) % NY, 0, 0)
            )
    weights = weights.reshape(2 * NZH * NY * rows, width)

    hidden = after(hidden, near_parts[1][2])
    h_sec = both(hidden, flip(hidden, 0, 1))
    h_all = jnp.concatenate([h_sec, flip(h_sec, 1, 0)], axis=1)
    teacher = teacher_half(codes, exponents)
    t_send = after(columns(teacher, 0, 1), near_parts[3][2])
    scaled_t = both(columns(teacher, 0, 0), flip(t_send, 0, 1))

    logits = jnp.dot(h_all, weights, preferred_element_type=jnp.float32)
    scaled_s = logits / TEMP
    m = jnp.max(scaled_s, axis=1)
    t_wide = scaled_t.astype(jnp.float32)
    t_exp = jnp.exp(t_wide)
    stats = jnp.stack(
        [
            m,
            jnp.sum(jnp.exp(scaled_s - m[:, None]), axis=1),
            jnp.sum(t_exp, axis=1),
            jnp.sum(t_exp * (t_wide - scaled_s), axis=1),
        ]
    ).reshape(8, tok)

    stats = jnp.stack([stats, flip(stats, 1, 0)])
    top = jnp.max(stats[:, 0:2], axis=0)
    s_sum = jnp.sum(stats[:, 2:4] * jnp.exp(stats[:, 0:2] - top), axis=0)
    rest = jnp.sum(stats[:, 4:8], axis=0)
    tiles = [
        jnp.concatenate([top, s_sum, rest[0:2], rest[2 + z : 3 + z], loss_weight[None]])
        for z in range(NZH)
    ]
    parts = jnp.broadcast_to(jnp.stack(tiles)[:, None], (NZH, NQ, 8, tok))
    parts = exchange(parts.reshape(NZH * NQ, 8, tok))
    top = jnp.max(parts[:, 0:2], axis=0)
    s_sum = jnp.sum(parts[:, 2:4] * jnp.exp(parts[:, 0:2] - top), axis=0)
    t_sum = jnp.sum(parts[:, 4:6], axis=0)
    cross = jnp.sum(parts[:, 6], axis=0)
    weight = jnp.concatenate([parts[0, 7], parts[NQ, 7]])
    student_lse = top + jnp.log(s_sum)
    teacher_lse = jnp.log(t_sum)

    def of_mine(a):
        return lax.dynamic_index_in_dim(a, zh, axis=0, keepdims=False)

    kl_loss = cross / of_mine(t_sum) - of_mine(teacher_lse) + of_mine(student_lse)
    kl_loss = TEMP * TEMP * kl_loss

    student_lse, teacher_lse = student_lse.reshape(2 * tok), teacher_lse.reshape(2 * tok)
    per_row = jnp.stack([student_lse, teacher_lse, weight], axis=1)
    w = weights.reshape(2, -1, width)
    feats = w.shape[1]
    logit_grad, g = in_vmem(
        first_grads_kernel,
        (scaled_s, scaled_t, per_row, w),
        (
            jax.ShapeDtypeStruct(scaled_s.shape, jnp.bfloat16),
            jax.ShapeDtypeStruct((NZH, feats, tok), jnp.bfloat16),
        ),
    )
    theirs = flip(g, 1, 0)
    (mine,) = in_vmem(
        second_grads_kernel,
        (logit_grad, w),
        (jax.ShapeDtypeStruct((NZH, feats, tok), jnp.float32),),
    )
    g = (mine + theirs.astype(jnp.float32)).astype(jnp.bfloat16)
    g = g.reshape(NZH * NQ, rows, tok)
    g = exchange(g)
    g = jnp.sum(g.astype(jnp.float32), axis=0)
    return (kl_loss, g.T.astype(jnp.bfloat16))


def solution(mesh):
    in_specs = (
        P("dp", "section"),
        P(("section", "dp"), "vocab"),
        P("dp", "vocab"),
        P("dp", "vocab"),
        P("dp"),
    )
    out_specs = (P("dp"), P("dp", ("section", "vocab")))
    return jax.shard_map(
        on_device, mesh=mesh, in_specs=in_specs, out_specs=out_specs, check_vma=False
    )
```

```python
import jax
import jax.numpy as jnp
from jax import lax
from jax.experimental import pallas as pl
from jax.experimental.pallas import tpu as pltpu
from jax.sharding import PartitionSpec as P

GROUP = 128
TEMP = 2
NY = 8
NZH = 2
NQ = 16


def flip(x, ds, dz):
    n = NZH * NY
    perm = []
    for s in range(2):
        for zh in range(NZH):
            for y in range(NY):
                perm.append((s * n + zh * NY + y, (s ^ ds) * n + (zh ^ dz) * NY + y))
    return lax.ppermute(x, ("section", "dp"), perm)


def along_y(x, step):
    perm = [(zh * NY + y, zh * NY + (y + step) % NY) for zh in range(NZH) for y in range(NY)]
    return lax.ppermute(x, "dp", perm)


def exchange(x):
    n = NZH * NY * NQ
    groups = [
        [s * n + (zh * NY + y) * NQ + q for zh in range(NZH) for q in range(NQ)]
        for s in range(2)
        for y in range(NY)
    ]
    return lax.all_to_all(
        x,
        ("section", "dp", "vocab"),
        split_axis=0,
        concat_axis=0,
        axis_index_groups=groups,
        tiled=True,
    )


def teacher_half(codes, exponents):
    rows, groups = exponents.shape
    scale = jnp.exp2(exponents.astype(jnp.float32)) / TEMP
    t = codes.astype(jnp.float32).reshape(rows, groups, GROUP) * scale[:, :, None]
    return t.reshape(rows, groups * GROUP).astype(jnp.bfloat16)


def after(x, *others):
    return lax.optimization_barrier((x,) + others)[0]


def ring(block):
    half = block.shape[0] // 2
    fwd, bwd = block, block
    parts = [(0, 0, block)]
    for step in range(1, NY // 2):
        fwd, bwd = along_y(fwd, 1), along_y(bwd, -1)
        parts.append((-step, 0, fwd))
        parts.append((step, 0, bwd))
    parts.append((NY // 2, 0, along_y(fwd[:half], 1)))
    parts.append((NY // 2, half, along_y(bwd[half:], -1)))
    return parts


TILE = 256


def grad_rows(w_ref, section, at, logit_grad):
    rows = w_ref[section, pl.ds(pl.multiple_of(at, TILE), TILE), :]
    return lax.dot_general(
        rows, logit_grad, (((1,), (1,)), ((), ())), preferred_element_type=jnp.float32
    )


def first_grads_kernel(s_ref, t_ref, row_ref, w_ref, lg_ref, g_ref):
    student_lse, teacher_lse, weight = row_ref[:, 0:1], row_ref[:, 1:2], row_ref[:, 2:3]
    student = jnp.exp(s_ref[...] - student_lse)
    teacher = jnp.exp(t_ref[...].astype(jnp.float32) - teacher_lse)
    lg_ref[...] = (weight * TEMP * (student - teacher)).astype(jnp.bfloat16)
    logit_grad = lg_ref[...]
    tok = g_ref.shape[2]

    def step(k, carry):
        g = grad_rows(w_ref, 1, k * TILE, logit_grad).astype(jnp.bfloat16)
        for z in range(NZH):
            g_ref[z, pl.ds(pl.multiple_of(k * TILE, TILE), TILE), :] = g[:, z * tok : (z + 1) * tok]
        return carry

    lax.fori_loop(0, g_ref.shape[1] // TILE, step, 0)


def second_grads_kernel(lg_ref, w_ref, g_ref):
    logit_grad = lg_ref[...]
    tok = g_ref.shape[2]

    def step(k, carry):
        g = grad_rows(w_ref, 0, k * TILE, logit_grad)
        for z in range(NZH):
            g_ref[z, pl.ds(pl.multiple_of(k * TILE, TILE), TILE), :] = g[:, z * tok : (z + 1) * tok]
        return carry

    lax.fori_loop(0, g_ref.shape[1] // TILE, step, 0)


def in_vmem(kernel, ins, outs):
    whole = pl.BlockSpec(memory_space=pltpu.VMEM)
    return pl.pallas_call(
        kernel,
        in_specs=[whole] * len(ins),
        out_specs=[whole] * len(outs),
        out_shape=outs,
        compiler_params=pltpu.CompilerParams(vmem_limit_bytes=4 * 2**20),
        cost_estimate=pl.CostEstimate(
            flops=10**9, bytes_accessed=5 * 10**6, transcendentals=5 * 10**5
        ),
    )(*ins)


def on_device(hidden, head, codes, exponents, loss_weight):
    s = lax.axis_index("section")
    dp = lax.axis_index("dp")
    zh, y = dp // NY, dp % NY
    rows, cols = head.shape
    width = cols // 4
    tok = hidden.shape[0]

    def columns(x, ds, dz):
        at = ((zh ^ dz) * 2 + (s ^ ds)) * width
        return lax.dynamic_slice_in_dim(x, at, width, axis=1)

    def both(mine, other):
        return jnp.where(
            zh == 0, jnp.concatenate([mine, other]), jnp.concatenate([other, mine])
        )

    near = jnp.concatenate([columns(head, 0, 0), flip(columns(head, 1, 0), 1, 0)], axis=0)
    near_parts = ring(near)
    away = lax.dynamic_slice_in_dim(head, (zh ^ 1) * 2 * width, 2 * width, axis=1)
    came = flip(away, 0, 1)
    came_mine = lax.dynamic_slice_in_dim(came, s * width, width, axis=1)
    came_send = lax.dynamic_slice_in_dim(came, (s ^ 1) * width, width, axis=1)
    far = jnp.concatenate([came_mine, flip(came_send, 1, 0)], axis=0)
    far_parts = ring(far)

    weights = jnp.zeros((2, NZH, NY, rows, width), head.dtype)
    for dz, parts in enumerate([near_parts, far_parts]):
        for dy, at, block in parts:
            block = block.reshape(-1, 1, 1, rows, width)
            weights = lax.dynamic_update_slice(
                weights, block, (at // rows, zh ^ dz, (y + dy) % NY, 0, 0)
            )
    weights = weights.reshape(2 * NZH * NY * rows, width)

    hidden = after(hidden, near_parts[1][2])
    h_sec = both(hidden, flip(hidden, 0, 1))
    h_all = jnp.concatenate([h_sec, flip(h_sec, 1, 0)], axis=1)
    teacher = teacher_half(codes, exponents)
    t_send = after(columns(teacher, 0, 1), near_parts[3][2])
    scaled_t = both(columns(teacher, 0, 0), flip(t_send, 0, 1))

    logits = jnp.dot(h_all, weights, preferred_element_type=jnp.float32)
    scaled_s = logits / TEMP
    m = jnp.max(scaled_s, axis=1)
    t_wide = scaled_t.astype(jnp.float32)
    t_exp = jnp.exp(t_wide)
    stats = jnp.stack(
        [
            m,
            jnp.sum(jnp.exp(scaled_s - m[:, None]), axis=1),
            jnp.sum(t_exp, axis=1),
            jnp.sum(t_exp * (t_wide - scaled_s), axis=1),
        ]
    ).reshape(8, tok)

    stats = jnp.stack([stats, flip(stats, 1, 0)])
    top = jnp.max(stats[:, 0:2], axis=0)
    s_sum = jnp.sum(stats[:, 2:4] * jnp.exp(stats[:, 0:2] - top), axis=0)
    rest = jnp.sum(stats[:, 4:8], axis=0)
    tiles = [
        jnp.concatenate([top, s_sum, rest[0:2], rest[2 + z : 3 + z], loss_weight[None]])
        for z in range(NZH)
    ]
    parts = jnp.broadcast_to(jnp.stack(tiles)[:, None], (NZH, NQ, 8, tok))
    parts = exchange(parts.reshape(NZH * NQ, 8, tok))
    top = jnp.max(parts[:, 0:2], axis=0)
    s_sum = jnp.sum(parts[:, 2:4] * jnp.exp(parts[:, 0:2] - top), axis=0)
    t_sum = jnp.sum(parts[:, 4:6], axis=0)
    cross = jnp.sum(parts[:, 6], axis=0)
    weight = jnp.concatenate([parts[0, 7], parts[NQ, 7]])
    student_lse = top + jnp.log(s_sum)
    teacher_lse = jnp.log(t_sum)

    def of_mine(a):
        return lax.dynamic_index_in_dim(a, zh, axis=0, keepdims=False)

    kl_loss = cross / of_mine(t_sum) - of_mine(teacher_lse) + of_mine(student_lse)
    kl_loss = TEMP * TEMP * kl_loss

    student_lse, teacher_lse = student_lse.reshape(2 * tok), teacher_lse.reshape(2 * tok)
    per_row = jnp.stack([student_lse, teacher_lse, weight], axis=1)
    w = weights.reshape(2, -1, width)
    feats = w.shape[1]
    logit_grad, g = in_vmem(
        first_grads_kernel,
        (scaled_s, scaled_t, per_row, w),
        (
            jax.ShapeDtypeStruct(scaled_s.shape, jnp.bfloat16),
            jax.ShapeDtypeStruct((NZH, feats, tok), jnp.bfloat16),
        ),
    )
    theirs = flip(g, 1, 0)
    (mine,) = in_vmem(
        second_grads_kernel,
        (logit_grad, w),
        (jax.ShapeDtypeStruct((NZH, feats, tok), jnp.float32),),
    )
    g = (mine + theirs.astype(jnp.float32)).astype(jnp.bfloat16)
    g = g.reshape(NZH * NQ, rows, tok)
    g = exchange(g)
    g = jnp.sum(g.astype(jnp.float32), axis=0)
    return (kl_loss, g.T.astype(jnp.bfloat16))


def solution(mesh):
    in_specs = (
        P("dp", "section"),
        P(("section", "dp"), "vocab"),
        P("dp", "vocab"),
        P("dp", "vocab"),
        P("dp"),
    )
    out_specs = (P("dp"), P("dp", ("section", "vocab")))
    return jax.shard_map(
        on_device, mesh=mesh, in_specs=in_specs, out_specs=out_specs, check_vma=False
    )
```

```python
import jax
import jax.numpy as jnp
from jax import lax
from jax.experimental import pallas as pl
from jax.experimental.pallas import tpu as pltpu
from jax.sharding import PartitionSpec as P

GROUP = 128
TEMP = 2
NY = 8
NZH = 2
NQ = 16


def flip(x, ds, dz):
    n = NZH * NY
    perm = []
    for s in range(2):
        for zh in range(NZH):
            for y in range(NY):
                perm.append((s * n + zh * NY + y, (s ^ ds) * n + (zh ^ dz) * NY + y))
    return lax.ppermute(x, ("section", "dp"), perm)


def along_y(x, step):
    perm = [(zh * NY + y, zh * NY + (y + step) % NY) for zh in range(NZH) for y in range(NY)]
    return lax.ppermute(x, "dp", perm)


def exchange(x):
    n = NZH * NY * NQ
    groups = [
        [s * n + (zh * NY + y) * NQ + q for zh in range(NZH) for q in range(NQ)]
        for s in range(2)
        for y in range(NY)
    ]
    return lax.all_to_all(
        x,
        ("section", "dp", "vocab"),
        split_axis=0,
        concat_axis=0,
        axis_index_groups=groups,
        tiled=True,
    )


def teacher_half(codes, exponents):
    rows, groups = exponents.shape
    scale = jnp.exp2(exponents.astype(jnp.float32)) / TEMP
    t = codes.astype(jnp.float32).reshape(rows, groups, GROUP) * scale[:, :, None]
    return t.reshape(rows, groups * GROUP).astype(jnp.bfloat16)


def after(x, *others):
    return lax.optimization_barrier((x,) + others)[0]


def ring(block):
    half = block.shape[0] // 2
    fwd, bwd = block, block
    parts = [(0, 0, block)]
    for step in range(1, NY // 2):
        fwd, bwd = along_y(fwd, 1), along_y(bwd, -1)
        parts.append((-step, 0, fwd))
        parts.append((step, 0, bwd))
    parts.append((NY // 2, 0, along_y(fwd[:half], 1)))
    parts.append((NY // 2, half, along_y(bwd[half:], -1)))
    return parts


TILE = 256


def tile_grads(w_ref, logit_grad, g_ref):
    g = lax.dot_general(
        w_ref[0], logit_grad, (((1,), (1,)), ((), ())), preferred_element_type=jnp.float32
    ).astype(g_ref.dtype)
    tok = g_ref.shape[2]
    for z in range(NZH):
        g_ref[z] = g[:, z * tok : (z + 1) * tok]


def first_grads_kernel(s_ref, t_ref, row_ref, w_ref, lg_ref, g_ref):
    @pl.when(pl.program_id(0) == 0)
    def _():
        student_lse, teacher_lse, weight = row_ref[:, 0:1], row_ref[:, 1:2], row_ref[:, 2:3]
        student = jnp.exp(s_ref[...] - student_lse)
        teacher = jnp.exp(t_ref[...].astype(jnp.float32) - teacher_lse)
        lg_ref[...] = (weight * TEMP * (student - teacher)).astype(jnp.bfloat16)

    tile_grads(w_ref, lg_ref[...], g_ref)


def second_grads_kernel(lg_ref, w_ref, g_ref):
    tile_grads(w_ref, lg_ref[...], g_ref)


def over_tiles(kernel, section, ins, weights, whole_outs, grads):
    whole = pl.BlockSpec(memory_space=pltpu.VMEM)
    width = weights.shape[2]
    zs, feats, tok = grads.shape
    return pl.pallas_call(
        kernel,
        grid=(feats // TILE,),
        in_specs=[whole] * len(ins) + [pl.BlockSpec((1, TILE, width), lambda k: (section, k, 0))],
        out_specs=[whole] * len(whole_outs) + [pl.BlockSpec((zs, TILE, tok), lambda k: (0, k, 0))],
        out_shape=[*whole_outs, grads],
        compiler_params=pltpu.CompilerParams(vmem_limit_bytes=16 * 2**20),
        cost_estimate=pl.CostEstimate(
            flops=10**9, bytes_accessed=5 * 10**6, transcendentals=5 * 10**5
        ),
    )(*ins, weights)


def on_device(hidden, head, codes, exponents, loss_weight):
    s = lax.axis_index("section")
    dp = lax.axis_index("dp")
    zh, y = dp // NY, dp % NY
    rows, cols = head.shape
    width = cols // 4
    tok = hidden.shape[0]

    def columns(x, ds, dz):
        at = ((zh ^ dz) * 2 + (s ^ ds)) * width
        return lax.dynamic_slice_in_dim(x, at, width, axis=1)

    def both(mine, other):
        return jnp.where(
            zh == 0, jnp.concatenate([mine, other]), jnp.concatenate([other, mine])
        )

    near = jnp.concatenate([columns(head, 0, 0), flip(columns(head, 1, 0), 1, 0)], axis=0)
    near_parts = ring(near)
    away = lax.dynamic_slice_in_dim(head, (zh ^ 1) * 2 * width, 2 * width, axis=1)
    came = flip(away, 0, 1)
    came_mine = lax.dynamic_slice_in_dim(came, s * width, width, axis=1)
    came_send = lax.dynamic_slice_in_dim(came, (s ^ 1) * width, width, axis=1)
    far = jnp.concatenate([came_mine, flip(came_send, 1, 0)], axis=0)
    far_parts = ring(far)

    weights = jnp.zeros((2, NZH, NY, rows, width), head.dtype)
    for dz, parts in enumerate([near_parts, far_parts]):
        for dy, at, block in parts:
            block = block.reshape(-1, 1, 1, rows, width)
            weights = lax.dynamic_update_slice(
                weights, block, (at // rows, zh ^ dz, (y + dy) % NY, 0, 0)
            )
    weights = weights.reshape(2 * NZH * NY * rows, width)

    hidden = after(hidden, near_parts[1][2])
    h_sec = both(hidden, flip(hidden, 0, 1))
    h_all = jnp.concatenate([h_sec, flip(h_sec, 1, 0)], axis=1)
    teacher = teacher_half(codes, exponents)
    t_send = after(columns(teacher, 0, 1), near_parts[3][2])
    scaled_t = both(columns(teacher, 0, 0), flip(t_send, 0, 1))

    logits = jnp.dot(h_all, weights, preferred_element_type=jnp.float32)
    scaled_s = logits / TEMP
    m = jnp.max(scaled_s, axis=1)
    t_wide = scaled_t.astype(jnp.float32)
    t_exp = jnp.exp(t_wide)
    stats = jnp.stack(
        [
            m,
            jnp.sum(jnp.exp(scaled_s - m[:, None]), axis=1),
            jnp.sum(t_exp, axis=1),
            jnp.sum(t_exp * (t_wide - scaled_s), axis=1),
        ]
    ).reshape(8, tok)

    stats = jnp.stack([stats, flip(stats, 1, 0)])
    top = jnp.max(stats[:, 0:2], axis=0)
    s_sum = jnp.sum(stats[:, 2:4] * jnp.exp(stats[:, 0:2] - top), axis=0)
    rest = jnp.sum(stats[:, 4:8], axis=0)
    tiles = [
        jnp.concatenate([top, s_sum, rest[0:2], rest[2 + z : 3 + z], loss_weight[None]])
        for z in range(NZH)
    ]
    parts = jnp.broadcast_to(jnp.stack(tiles)[:, None], (NZH, NQ, 8, tok))
    parts = exchange(parts.reshape(NZH * NQ, 8, tok))
    top = jnp.max(parts[:, 0:2], axis=0)
    s_sum = jnp.sum(parts[:, 2:4] * jnp.exp(parts[:, 0:2] - top), axis=0)
    t_sum = jnp.sum(parts[:, 4:6], axis=0)
    cross = jnp.sum(parts[:, 6], axis=0)
    weight = jnp.concatenate([parts[0, 7], parts[NQ, 7]])
    student_lse = top + jnp.log(s_sum)
    teacher_lse = jnp.log(t_sum)

    def of_mine(a):
        return lax.dynamic_index_in_dim(a, zh, axis=0, keepdims=False)

    kl_loss = cross / of_mine(t_sum) - of_mine(teacher_lse) + of_mine(student_lse)
    kl_loss = TEMP * TEMP * kl_loss

    student_lse, teacher_lse = student_lse.reshape(2 * tok), teacher_lse.reshape(2 * tok)
    per_row = jnp.stack([student_lse, teacher_lse, weight], axis=1)
    w = weights.reshape(2, -1, width)
    feats = w.shape[1]
    logit_grad, g = over_tiles(
        first_grads_kernel,
        1,
        (scaled_s, scaled_t, per_row),
        w,
        [jax.ShapeDtypeStruct(scaled_s.shape, jnp.bfloat16)],
        jax.ShapeDtypeStruct((NZH, feats, tok), jnp.bfloat16),
    )
    theirs = flip(g, 1, 0)
    (mine,) = over_tiles(
        second_grads_kernel,
        0,
        (logit_grad,),
        w,
        [],
        jax.ShapeDtypeStruct((NZH, feats, tok), jnp.float32),
    )
    g = (mine + theirs.astype(jnp.float32)).astype(jnp.bfloat16)
    g = g.reshape(NZH * NQ, rows, tok)
    g = exchange(g)
    g = jnp.sum(g.astype(jnp.float32), axis=0)
    return (kl_loss, g.T.astype(jnp.bfloat16))


def solution(mesh):
    in_specs = (
        P("dp", "section"),
        P(("section", "dp"), "vocab"),
        P("dp", "vocab"),
        P("dp", "vocab"),
        P("dp"),
    )
    out_specs = (P("dp"), P("dp", ("section", "vocab")))
    return jax.shard_map(
        on_device, mesh=mesh, in_specs=in_specs, out_specs=out_specs, check_vma=False
    )
```

```python
import jax
import jax.numpy as jnp
from jax import lax
from jax.experimental import pallas as pl
from jax.experimental.pallas import tpu as pltpu
from jax.sharding import PartitionSpec as P

GROUP = 128
TEMP = 2
NY = 8
NZH = 2
NQ = 16


def flip(x, ds, dz):
    n = NZH * NY
    perm = []
    for s in range(2):
        for zh in range(NZH):
            for y in range(NY):
                perm.append((s * n + zh * NY + y, (s ^ ds) * n + (zh ^ dz) * NY + y))
    return lax.ppermute(x, ("section", "dp"), perm)


def along_y(x, step):
    perm = [(zh * NY + y, zh * NY + (y + step) % NY) for zh in range(NZH) for y in range(NY)]
    return lax.ppermute(x, "dp", perm)


def exchange(x):
    n = NZH * NY * NQ
    groups = [
        [s * n + (zh * NY + y) * NQ + q for zh in range(NZH) for q in range(NQ)]
        for s in range(2)
        for y in range(NY)
    ]
    return lax.all_to_all(
        x,
        ("section", "dp", "vocab"),
        split_axis=0,
        concat_axis=0,
        axis_index_groups=groups,
        tiled=True,
    )


def teacher_half(codes, exponents):
    rows, groups = exponents.shape
    scale = jnp.exp2(exponents.astype(jnp.float32)) / TEMP
    t = codes.astype(jnp.float32).reshape(rows, groups, GROUP) * scale[:, :, None]
    return t.reshape(rows, groups * GROUP).astype(jnp.bfloat16)


def after(x, *others):
    return lax.optimization_barrier((x,) + others)[0]


def ring(block):
    half = block.shape[0] // 2
    fwd, bwd = block, block
    parts = [(0, 0, block)]
    for step in range(1, NY // 2):
        fwd, bwd = along_y(fwd, 1), along_y(bwd, -1)
        parts.append((-step, 0, fwd))
        parts.append((step, 0, bwd))
    parts.append((NY // 2, 0, along_y(fwd[:half], 1)))
    parts.append((NY // 2, half, along_y(bwd[half:], -1)))
    return parts


TILE = 256


def tile_grads(w_ref, logit_grad, g_ref):
    g = lax.dot_general(
        w_ref[0], logit_grad, (((1,), (1,)), ((), ())), preferred_element_type=jnp.float32
    ).astype(g_ref.dtype)
    tok = g_ref.shape[2]
    for z in range(NZH):
        g_ref[z] = g[:, z * tok : (z + 1) * tok]


def first_grads_kernel(s_ref, t_ref, row_ref, w_ref, lg_ref, g_ref):
    @pl.when(pl.program_id(0) == 0)
    def _():
        student_lse, teacher_lse, weight = row_ref[:, 0:1], row_ref[:, 1:2], row_ref[:, 2:3]
        student = jnp.exp(s_ref[...] - student_lse)
        teacher = jnp.exp(t_ref[...].astype(jnp.float32) - teacher_lse)
        lg_ref[...] = (weight * TEMP * (student - teacher)).astype(jnp.bfloat16)

    tile_grads(w_ref, lg_ref[...], g_ref)


def second_grads_kernel(lg_ref, w_ref, g_ref):
    tile_grads(w_ref, lg_ref[...], g_ref)


def over_tiles(kernel, section, ins, weights, whole_outs, grads):
    whole = pl.BlockSpec(memory_space=pltpu.VMEM)
    width = weights.shape[2]
    zs, feats, tok = grads.shape
    return pl.pallas_call(
        kernel,
        grid=(feats // TILE,),
        in_specs=[whole] * len(ins) + [pl.BlockSpec((1, TILE, width), lambda k: (section, k, 0))],
        out_specs=[whole] * len(whole_outs) + [pl.BlockSpec((zs, TILE, tok), lambda k: (0, k, 0))],
        out_shape=[*whole_outs, grads],
        compiler_params=pltpu.CompilerParams(vmem_limit_bytes=58 * 2**20),
        cost_estimate=pl.CostEstimate(
            flops=10**9, bytes_accessed=5 * 10**6, transcendentals=5 * 10**5
        ),
    )(*ins, weights)


def on_device(hidden, head, codes, exponents, loss_weight):
    s = lax.axis_index("section")
    dp = lax.axis_index("dp")
    zh, y = dp // NY, dp % NY
    rows, cols = head.shape
    width = cols // 4
    tok = hidden.shape[0]

    def columns(x, ds, dz):
        at = ((zh ^ dz) * 2 + (s ^ ds)) * width
        return lax.dynamic_slice_in_dim(x, at, width, axis=1)

    def both(mine, other):
        return jnp.where(
            zh == 0, jnp.concatenate([mine, other]), jnp.concatenate([other, mine])
        )

    near = jnp.concatenate([columns(head, 0, 0), flip(columns(head, 1, 0), 1, 0)], axis=0)
    near_parts = ring(near)
    away = lax.dynamic_slice_in_dim(head, (zh ^ 1) * 2 * width, 2 * width, axis=1)
    came = flip(away, 0, 1)
    came_mine = lax.dynamic_slice_in_dim(came, s * width, width, axis=1)
    came_send = lax.dynamic_slice_in_dim(came, (s ^ 1) * width, width, axis=1)
    far = jnp.concatenate([came_mine, flip(came_send, 1, 0)], axis=0)
    far_parts = ring(far)

    weights = jnp.zeros((2, NZH, NY, rows, width), head.dtype)
    for dz, parts in enumerate([near_parts, far_parts]):
        for dy, at, block in parts:
            block = block.reshape(-1, 1, 1, rows, width)
            weights = lax.dynamic_update_slice(
                weights, block, (at // rows, zh ^ dz, (y + dy) % NY, 0, 0)
            )
    weights = weights.reshape(2 * NZH * NY * rows, width)

    hidden = after(hidden, near_parts[1][2])
    h_sec = both(hidden, flip(hidden, 0, 1))
    h_all = jnp.concatenate([h_sec, flip(h_sec, 1, 0)], axis=1)
    teacher = teacher_half(codes, exponents)
    t_send = after(columns(teacher, 0, 1), near_parts[3][2])
    scaled_t = both(columns(teacher, 0, 0), flip(t_send, 0, 1))

    logits = jnp.dot(h_all, weights, preferred_element_type=jnp.float32)
    scaled_s = logits / TEMP
    m = jnp.max(scaled_s, axis=1)
    t_wide = scaled_t.astype(jnp.float32)
    t_exp = jnp.exp(t_wide)
    stats = jnp.stack(
        [
            m,
            jnp.sum(jnp.exp(scaled_s - m[:, None]), axis=1),
            jnp.sum(t_exp, axis=1),
            jnp.sum(t_exp * (t_wide - scaled_s), axis=1),
        ]
    ).reshape(8, tok)

    stats = jnp.stack([stats, flip(stats, 1, 0)])
    top = jnp.max(stats[:, 0:2], axis=0)
    s_sum = jnp.sum(stats[:, 2:4] * jnp.exp(stats[:, 0:2] - top), axis=0)
    rest = jnp.sum(stats[:, 4:8], axis=0)
    tiles = [
        jnp.concatenate([top, s_sum, rest[0:2], rest[2 + z : 3 + z], loss_weight[None]])
        for z in range(NZH)
    ]
    parts = jnp.broadcast_to(jnp.stack(tiles)[:, None], (NZH, NQ, 8, tok))
    parts = exchange(parts.reshape(NZH * NQ, 8, tok))
    top = jnp.max(parts[:, 0:2], axis=0)
    s_sum = jnp.sum(parts[:, 2:4] * jnp.exp(parts[:, 0:2] - top), axis=0)
    t_sum = jnp.sum(parts[:, 4:6], axis=0)
    cross = jnp.sum(parts[:, 6], axis=0)
    weight = jnp.concatenate([parts[0, 7], parts[NQ, 7]])
    student_lse = top + jnp.log(s_sum)
    teacher_lse = jnp.log(t_sum)

    def of_mine(a):
        return lax.dynamic_index_in_dim(a, zh, axis=0, keepdims=False)

    kl_loss = cross / of_mine(t_sum) - of_mine(teacher_lse) + of_mine(student_lse)
    kl_loss = TEMP * TEMP * kl_loss

    student_lse, teacher_lse = student_lse.reshape(2 * tok), teacher_lse.reshape(2 * tok)
    per_row = jnp.stack([student_lse, teacher_lse, weight], axis=1)
    w = weights.reshape(2, -1, width)
    feats = w.shape[1]
    logit_grad, g = over_tiles(
        first_grads_kernel,
        1,
        (scaled_s, scaled_t, per_row),
        w,
        [jax.ShapeDtypeStruct(scaled_s.shape, jnp.bfloat16)],
        jax.ShapeDtypeStruct((NZH, feats, tok), jnp.bfloat16),
    )
    theirs = flip(g, 1, 0)
    (mine,) = over_tiles(
        second_grads_kernel,
        0,
        (logit_grad,),
        w,
        [],
        jax.ShapeDtypeStruct((NZH, feats, tok), jnp.float32),
    )
    g = (mine + theirs.astype(jnp.float32)).astype(jnp.bfloat16)
    g = g.reshape(NZH * NQ, rows, tok)
    g = exchange(g)
    g = jnp.sum(g.astype(jnp.float32), axis=0)
    return (kl_loss, g.T.astype(jnp.bfloat16))


def solution(mesh):
    in_specs = (
        P("dp", "section"),
        P(("section", "dp"), "vocab"),
        P("dp", "vocab"),
        P("dp", "vocab"),
        P("dp"),
    )
    out_specs = (P("dp"), P("dp", ("section", "vocab")))
    return jax.shard_map(
        on_device, mesh=mesh, in_specs=in_specs, out_specs=out_specs, check_vma=False
    )
```

```python
import jax
import jax.numpy as jnp
from jax import lax
from jax.experimental import pallas as pl
from jax.experimental.pallas import tpu as pltpu
from jax.sharding import PartitionSpec as P

GROUP = 128
TEMP = 2
NY = 8
NZH = 2
NQ = 16


def flip(x, ds, dz):
    n = NZH * NY
    perm = []
    for s in range(2):
        for zh in range(NZH):
            for y in range(NY):
                perm.append((s * n + zh * NY + y, (s ^ ds) * n + (zh ^ dz) * NY + y))
    return lax.ppermute(x, ("section", "dp"), perm)


def along_y(x, step):
    perm = [(zh * NY + y, zh * NY + (y + step) % NY) for zh in range(NZH) for y in range(NY)]
    return lax.ppermute(x, "dp", perm)


def exchange(x):
    n = NZH * NY * NQ
    groups = [
        [s * n + (zh * NY + y) * NQ + q for zh in range(NZH) for q in range(NQ)]
        for s in range(2)
        for y in range(NY)
    ]
    return lax.all_to_all(
        x,
        ("section", "dp", "vocab"),
        split_axis=0,
        concat_axis=0,
        axis_index_groups=groups,
        tiled=True,
    )


def teacher_half(codes, exponents):
    rows, groups = exponents.shape
    scale = jnp.exp2(exponents.astype(jnp.float32)) / TEMP
    t = codes.astype(jnp.float32).reshape(rows, groups, GROUP) * scale[:, :, None]
    return t.reshape(rows, groups * GROUP).astype(jnp.bfloat16)


def after(x, *others):
    return lax.optimization_barrier((x,) + others)[0]


def ring(block):
    half = block.shape[0] // 2
    fwd, bwd = block, block
    parts = [(0, 0, block)]
    for step in range(1, NY // 2):
        fwd, bwd = along_y(fwd, 1), along_y(bwd, -1)
        parts.append((-step, 0, fwd))
        parts.append((step, 0, bwd))
    parts.append((NY // 2, 0, along_y(fwd[:half], 1)))
    parts.append((NY // 2, half, along_y(bwd[half:], -1)))
    return parts


TILE = 256


def tile_grads(w_ref, logit_grad, g_ref):
    g = lax.dot_general(
        w_ref[0], logit_grad, (((1,), (1,)), ((), ())), preferred_element_type=jnp.float32
    ).astype(g_ref.dtype)
    tok = g_ref.shape[2]
    for z in range(NZH):
        g_ref[z] = g[:, z * tok : (z + 1) * tok]


def exps_kernel(s_ref, t_ref, m_ref, es_ref, et_ref):
    es_ref[...] = jnp.exp(s_ref[...] - m_ref[...])
    et_ref[...] = jnp.exp(t_ref[...].astype(jnp.float32))


def exps(scaled_s, scaled_t, m):
    whole = pl.BlockSpec(memory_space=pltpu.VMEM)
    out = jax.ShapeDtypeStruct(scaled_s.shape, jnp.float32)
    return pl.pallas_call(
        exps_kernel,
        in_specs=[whole] * 3,
        out_specs=[whole] * 2,
        out_shape=[out, out],
        compiler_params=pltpu.CompilerParams(vmem_limit_bytes=16 * 2**20),
        cost_estimate=pl.CostEstimate(
            flops=10**6, bytes_accessed=4 * 10**6, transcendentals=5 * 10**5
        ),
    )(scaled_s, scaled_t, m)


def first_grads_kernel(es_ref, et_ref, row_ref, w_ref, lg_ref, g_ref):
    @pl.when(pl.program_id(0) == 0)
    def _():
        student, teacher, weight = row_ref[:, 0:1], row_ref[:, 1:2], row_ref[:, 2:3]
        grad = es_ref[...] * student - et_ref[...] * teacher
        lg_ref[...] = (weight * TEMP * grad).astype(jnp.bfloat16)

    tile_grads(w_ref, lg_ref[...], g_ref)


def second_grads_kernel(lg_ref, w_ref, g_ref):
    tile_grads(w_ref, lg_ref[...], g_ref)


def over_tiles(kernel, section, ins, weights, whole_outs, grads):
    whole = pl.BlockSpec(memory_space=pltpu.VMEM)
    width = weights.shape[2]
    zs, feats, tok = grads.shape
    return pl.pallas_call(
        kernel,
        grid=(feats // TILE,),
        in_specs=[whole] * len(ins) + [pl.BlockSpec((1, TILE, width), lambda k: (section, k, 0))],
        out_specs=[whole] * len(whole_outs) + [pl.BlockSpec((zs, TILE, tok), lambda k: (0, k, 0))],
        out_shape=[*whole_outs, grads],
        compiler_params=pltpu.CompilerParams(vmem_limit_bytes=16 * 2**20),
        cost_estimate=pl.CostEstimate(
            flops=10**9, bytes_accessed=5 * 10**6, transcendentals=5 * 10**5
        ),
    )(*ins, weights)


def on_device(hidden, head, codes, exponents, loss_weight):
    s = lax.axis_index("section")
    dp = lax.axis_index("dp")
    zh, y = dp // NY, dp % NY
    rows, cols = head.shape
    width = cols // 4
    tok = hidden.shape[0]

    def columns(x, ds, dz):
        at = ((zh ^ dz) * 2 + (s ^ ds)) * width
        return lax.dynamic_slice_in_dim(x, at, width, axis=1)

    def both(mine, other):
        return jnp.where(
            zh == 0, jnp.concatenate([mine, other]), jnp.concatenate([other, mine])
        )

    near = jnp.concatenate([columns(head, 0, 0), flip(columns(head, 1, 0), 1, 0)], axis=0)
    near_parts = ring(near)
    away = lax.dynamic_slice_in_dim(head, (zh ^ 1) * 2 * width, 2 * width, axis=1)
    came = flip(away, 0, 1)
    came_mine = lax.dynamic_slice_in_dim(came, s * width, width, axis=1)
    came_send = lax.dynamic_slice_in_dim(came, (s ^ 1) * width, width, axis=1)
    far = jnp.concatenate([came_mine, flip(came_send, 1, 0)], axis=0)
    far_parts = ring(far)

    weights = jnp.zeros((2, NZH, NY, rows, width), head.dtype)
    for dz, parts in enumerate([near_parts, far_parts]):
        for dy, at, block in parts:
            block = block.reshape(-1, 1, 1, rows, width)
            weights = lax.dynamic_update_slice(
                weights, block, (at // rows, zh ^ dz, (y + dy) % NY, 0, 0)
            )
    weights = weights.reshape(2 * NZH * NY * rows, width)

    hidden = after(hidden, near_parts[1][2])
    h_sec = both(hidden, flip(hidden, 0, 1))
    h_all = jnp.concatenate([h_sec, flip(h_sec, 1, 0)], axis=1)
    teacher = teacher_half(codes, exponents)
    t_send = after(columns(teacher, 0, 1), near_parts[3][2])
    scaled_t = both(columns(teacher, 0, 0), flip(t_send, 0, 1))

    logits = jnp.dot(h_all, weights, preferred_element_type=jnp.float32)
    scaled_s = logits / TEMP
    m = jnp.max(scaled_s, axis=1)
    t_wide = scaled_t.astype(jnp.float32)
    t_exp = jnp.exp(t_wide)
    stats = jnp.stack(
        [
            m,
            jnp.sum(jnp.exp(scaled_s - m[:, None]), axis=1),
            jnp.sum(t_exp, axis=1),
            jnp.sum(t_exp * (t_wide - scaled_s), axis=1),
        ]
    ).reshape(8, tok)

    stats = jnp.stack([stats, flip(stats, 1, 0)])
    top = jnp.max(stats[:, 0:2], axis=0)
    s_sum = jnp.sum(stats[:, 2:4] * jnp.exp(stats[:, 0:2] - top), axis=0)
    rest = jnp.sum(stats[:, 4:8], axis=0)
    tiles = [
        jnp.concatenate([top, s_sum, rest[0:2], rest[2 + z : 3 + z], loss_weight[None]])
        for z in range(NZH)
    ]
    parts = jnp.broadcast_to(jnp.stack(tiles)[:, None], (NZH, NQ, 8, tok))
    parts = parts.reshape(NZH * NQ, 8, tok)
    e_student, e_teacher = exps(after(scaled_s, parts), scaled_t, m[:, None])
    parts = exchange(parts)
    top = jnp.max(parts[:, 0:2], axis=0)
    s_sum = jnp.sum(parts[:, 2:4] * jnp.exp(parts[:, 0:2] - top), axis=0)
    t_sum = jnp.sum(parts[:, 4:6], axis=0)
    cross = jnp.sum(parts[:, 6], axis=0)
    weight = jnp.concatenate([parts[0, 7], parts[NQ, 7]])
    student_lse = top + jnp.log(s_sum)
    teacher_lse = jnp.log(t_sum)

    def of_mine(a):
        return lax.dynamic_index_in_dim(a, zh, axis=0, keepdims=False)

    kl_loss = cross / of_mine(t_sum) - of_mine(teacher_lse) + of_mine(student_lse)
    kl_loss = TEMP * TEMP * kl_loss

    student_lse, teacher_lse = student_lse.reshape(2 * tok), teacher_lse.reshape(2 * tok)
    per_row = jnp.stack([jnp.exp(m - student_lse), jnp.exp(-teacher_lse), weight], axis=1)
    w = weights.reshape(2, -1, width)
    feats = w.shape[1]
    logit_grad, g = over_tiles(
        first_grads_kernel,
        1,
        (e_student, e_teacher, per_row),
        w,
        [jax.ShapeDtypeStruct(scaled_s.shape, jnp.bfloat16)],
        jax.ShapeDtypeStruct((NZH, feats, tok), jnp.bfloat16),
    )
    theirs = flip(g, 1, 0)
    (mine,) = over_tiles(
        second_grads_kernel,
        0,
        (logit_grad,),
        w,
        [],
        jax.ShapeDtypeStruct((NZH, feats, tok), jnp.float32),
    )
    g = (mine + theirs.astype(jnp.float32)).astype(jnp.bfloat16)
    g = g.reshape(NZH * NQ, rows, tok)
    g = exchange(g)
    g = jnp.sum(g.astype(jnp.float32), axis=0)
    return (kl_loss, g.T.astype(jnp.bfloat16))


def solution(mesh):
    in_specs = (
        P("dp", "section"),
        P(("section", "dp"), "vocab"),
        P("dp", "vocab"),
        P("dp", "vocab"),
        P("dp"),
    )
    out_specs = (P("dp"), P("dp", ("section", "vocab")))
    return jax.shard_map(
        on_device, mesh=mesh, in_specs=in_specs, out_specs=out_specs, check_vma=False
    )
```

```python
import jax
import jax.numpy as jnp
from jax import lax
from jax.experimental import pallas as pl
from jax.experimental.pallas import tpu as pltpu
from jax.sharding import PartitionSpec as P

GROUP = 128
TEMP = 2
NY = 8
NZH = 2
NQ = 16


def flip(x, ds, dz):
    n = NZH * NY
    perm = []
    for s in range(2):
        for zh in range(NZH):
            for y in range(NY):
                perm.append((s * n + zh * NY + y, (s ^ ds) * n + (zh ^ dz) * NY + y))
    return lax.ppermute(x, ("section", "dp"), perm)


def along_y(x, step):
    perm = [(zh * NY + y, zh * NY + (y + step) % NY) for zh in range(NZH) for y in range(NY)]
    return lax.ppermute(x, "dp", perm)


def exchange(x):
    n = NZH * NY * NQ
    groups = [
        [s * n + (zh * NY + y) * NQ + q for zh in range(NZH) for q in range(NQ)]
        for s in range(2)
        for y in range(NY)
    ]
    return lax.all_to_all(
        x,
        ("section", "dp", "vocab"),
        split_axis=0,
        concat_axis=0,
        axis_index_groups=groups,
        tiled=True,
    )


def teacher_half(codes, exponents):
    rows, groups = exponents.shape
    scale = jnp.exp2(exponents.astype(jnp.float32)) / TEMP
    t = codes.astype(jnp.float32).reshape(rows, groups, GROUP) * scale[:, :, None]
    return t.reshape(rows, groups * GROUP).astype(jnp.bfloat16)


def after(x, *others):
    return lax.optimization_barrier((x,) + others)[0]


def ring(block):
    half = block.shape[0] // 2
    fwd, bwd = block, block
    parts = [(0, 0, block)]
    for step in range(1, NY // 2):
        fwd, bwd = along_y(fwd, 1), along_y(bwd, -1)
        parts.append((-step, 0, fwd))
        parts.append((step, 0, bwd))
    parts.append((NY // 2, 0, along_y(fwd[:half], 1)))
    parts.append((NY // 2, half, along_y(bwd[half:], -1)))
    return parts


TILE = 256


def tile_grads(w_ref, logit_grad, g_ref):
    g = lax.dot_general(
        w_ref[0], logit_grad, (((1,), (1,)), ((), ())), preferred_element_type=jnp.float32
    ).astype(g_ref.dtype)
    tok = g_ref.shape[2]
    for z in range(NZH):
        g_ref[z] = g[:, z * tok : (z + 1) * tok]


def first_grads_kernel(s_ref, t_ref, row_ref, w_ref, lg_ref, g_ref):
    @pl.when(pl.program_id(0) == 0)
    def _():
        student_lse, teacher_lse, weight = row_ref[:, 0:1], row_ref[:, 1:2], row_ref[:, 2:3]
        student = jnp.exp(s_ref[...] - student_lse)
        teacher = jnp.exp(t_ref[...].astype(jnp.float32) - teacher_lse)
        lg_ref[...] = (weight * TEMP * (student - teacher)).astype(jnp.bfloat16)

    tile_grads(w_ref, lg_ref[...], g_ref)


def second_grads_kernel(lg_ref, w_ref, g_ref):
    tile_grads(w_ref, lg_ref[...], g_ref)


def over_tiles(kernel, section, ins, weights, whole_outs, grads):
    whole = pl.BlockSpec(memory_space=pltpu.VMEM)
    width = weights.shape[2]
    zs, feats, tok = grads.shape
    return pl.pallas_call(
        kernel,
        grid=(feats // TILE,),
        in_specs=[whole] * len(ins) + [pl.BlockSpec((1, TILE, width), lambda k: (section, k, 0))],
        out_specs=[whole] * len(whole_outs) + [pl.BlockSpec((zs, TILE, tok), lambda k: (0, k, 0))],
        out_shape=[*whole_outs, grads],
        compiler_params=pltpu.CompilerParams(vmem_limit_bytes=16 * 2**20),
        cost_estimate=pl.CostEstimate(
            flops=10**9, bytes_accessed=5 * 10**6, transcendentals=5 * 10**5
        ),
    )(*ins, weights)


def on_device(hidden, head, codes, exponents, loss_weight):
    s = lax.axis_index("section")
    dp = lax.axis_index("dp")
    zh, y = dp // NY, dp % NY
    rows, cols = head.shape
    width = cols // 4
    tok = hidden.shape[0]

    def columns(x, ds, dz):
        at = ((zh ^ dz) * 2 + (s ^ ds)) * width
        return lax.dynamic_slice_in_dim(x, at, width, axis=1)

    def both(mine, other):
        return jnp.where(
            zh == 0, jnp.concatenate([mine, other]), jnp.concatenate([other, mine])
        )

    away = lax.dynamic_slice_in_dim(head, (zh ^ 1) * 2 * width, 2 * width, axis=1)
    first = after(head, away)
    near = jnp.concatenate([columns(first, 0, 0), flip(columns(first, 1, 0), 1, 0)], axis=0)
    near_parts = ring(near)
    came = flip(away, 0, 1)
    came_mine = lax.dynamic_slice_in_dim(came, s * width, width, axis=1)
    came_send = lax.dynamic_slice_in_dim(came, (s ^ 1) * width, width, axis=1)
    far = jnp.concatenate([came_mine, flip(came_send, 1, 0)], axis=0)
    far_parts = ring(far)

    weights = jnp.zeros((2, NZH, NY, rows, width), head.dtype)
    for dz, parts in enumerate([near_parts, far_parts]):
        for dy, at, block in parts:
            block = block.reshape(-1, 1, 1, rows, width)
            weights = lax.dynamic_update_slice(
                weights, block, (at // rows, zh ^ dz, (y + dy) % NY, 0, 0)
            )
    weights = weights.reshape(2 * NZH * NY * rows, width)

    hidden = after(hidden, near_parts[1][2])
    h_sec = both(hidden, flip(hidden, 0, 1))
    h_all = jnp.concatenate([h_sec, flip(h_sec, 1, 0)], axis=1)
    teacher = teacher_half(codes, exponents)
    t_send = after(columns(teacher, 0, 1), near_parts[3][2])
    scaled_t = both(columns(teacher, 0, 0), flip(t_send, 0, 1))

    logits = jnp.dot(h_all, weights, preferred_element_type=jnp.float32)
    scaled_s = logits / TEMP
    m = jnp.max(scaled_s, axis=1)
    t_wide = scaled_t.astype(jnp.float32)
    t_exp = jnp.exp(t_wide)
    stats = jnp.stack(
        [
            m,
            jnp.sum(jnp.exp(scaled_s - m[:, None]), axis=1),
            jnp.sum(t_exp, axis=1),
            jnp.sum(t_exp * (t_wide - scaled_s), axis=1),
        ]
    ).reshape(8, tok)

    stats = jnp.stack([stats, flip(stats, 1, 0)])
    top = jnp.max(stats[:, 0:2], axis=0)
    s_sum = jnp.sum(stats[:, 2:4] * jnp.exp(stats[:, 0:2] - top), axis=0)
    rest = jnp.sum(stats[:, 4:8], axis=0)
    tiles = [
        jnp.concatenate([top, s_sum, rest[0:2], rest[2 + z : 3 + z], loss_weight[None]])
        for z in range(NZH)
    ]
    parts = jnp.broadcast_to(jnp.stack(tiles)[:, None], (NZH, NQ, 8, tok))
    parts = exchange(parts.reshape(NZH * NQ, 8, tok))
    top = jnp.max(parts[:, 0:2], axis=0)
    s_sum = jnp.sum(parts[:, 2:4] * jnp.exp(parts[:, 0:2] - top), axis=0)
    t_sum = jnp.sum(parts[:, 4:6], axis=0)
    cross = jnp.sum(parts[:, 6], axis=0)
    weight = jnp.concatenate([parts[0, 7], parts[NQ, 7]])
    student_lse = top + jnp.log(s_sum)
    teacher_lse = jnp.log(t_sum)

    def of_mine(a):
        return lax.dynamic_index_in_dim(a, zh, axis=0, keepdims=False)

    kl_loss = cross / of_mine(t_sum) - of_mine(teacher_lse) + of_mine(student_lse)
    kl_loss = TEMP * TEMP * kl_loss

    student_lse, teacher_lse = student_lse.reshape(2 * tok), teacher_lse.reshape(2 * tok)
    per_row = jnp.stack([student_lse, teacher_lse, weight], axis=1)
    w = weights.reshape(2, -1, width)
    feats = w.shape[1]
    logit_grad, g = over_tiles(
        first_grads_kernel,
        1,
        (scaled_s, scaled_t, per_row),
        w,
        [jax.ShapeDtypeStruct(scaled_s.shape, jnp.bfloat16)],
        jax.ShapeDtypeStruct((NZH, feats, tok), jnp.bfloat16),
    )
    theirs = flip(g, 1, 0)
    (mine,) = over_tiles(
        second_grads_kernel,
        0,
        (logit_grad,),
        w,
        [],
        jax.ShapeDtypeStruct((NZH, feats, tok), jnp.float32),
    )
    g = (mine + theirs.astype(jnp.float32)).astype(jnp.bfloat16)
    g = g.reshape(NZH * NQ, rows, tok)
    g = exchange(g)
    g = jnp.sum(g.astype(jnp.float32), axis=0)
    return (kl_loss, g.T.astype(jnp.bfloat16))


def solution(mesh):
    in_specs = (
        P("dp", "section"),
        P(("section", "dp"), "vocab"),
        P("dp", "vocab"),
        P("dp", "vocab"),
        P("dp"),
    )
    out_specs = (P("dp"), P("dp", ("section", "vocab")))
    return jax.shard_map(
        on_device, mesh=mesh, in_specs=in_specs, out_specs=out_specs, check_vma=False
    )
```

```python
import jax
import jax.numpy as jnp
from jax import lax
from jax.experimental import pallas as pl
from jax.experimental.pallas import tpu as pltpu
from jax.sharding import PartitionSpec as P

GROUP = 128
TEMP = 2
NY = 8
NZH = 2
NQ = 16


def flip(x, ds, dz):
    n = NZH * NY
    perm = []
    for s in range(2):
        for zh in range(NZH):
            for y in range(NY):
                perm.append((s * n + zh * NY + y, (s ^ ds) * n + (zh ^ dz) * NY + y))
    return lax.ppermute(x, ("section", "dp"), perm)


def along_y(x, step):
    perm = [(zh * NY + y, zh * NY + (y + step) % NY) for zh in range(NZH) for y in range(NY)]
    return lax.ppermute(x, "dp", perm)


def exchange(x):
    n = NZH * NY * NQ
    groups = [
        [s * n + (zh * NY + y) * NQ + q for zh in range(NZH) for q in range(NQ)]
        for s in range(2)
        for y in range(NY)
    ]
    return lax.all_to_all(
        x,
        ("section", "dp", "vocab"),
        split_axis=0,
        concat_axis=0,
        axis_index_groups=groups,
        tiled=True,
    )


def teacher_half(codes, exponents):
    rows, groups = exponents.shape
    scale = jnp.exp2(exponents.astype(jnp.float32)) / TEMP
    t = codes.astype(jnp.float32).reshape(rows, groups, GROUP) * scale[:, :, None]
    return t.reshape(rows, groups * GROUP).astype(jnp.bfloat16)


def after(x, *others):
    return lax.optimization_barrier((x,) + others)[0]


def ring(block):
    half = block.shape[0] // 2
    fwd, bwd = block, block
    parts = [(0, 0, block)]
    for step in range(1, NY // 2):
        fwd, bwd = along_y(fwd, 1), along_y(bwd, -1)
        parts.append((-step, 0, fwd))
        parts.append((step, 0, bwd))
    parts.append((NY // 2, 0, along_y(fwd[:half], 1)))
    parts.append((NY // 2, half, along_y(bwd[half:], -1)))
    return parts


TILE = 256


def tile_grads(w_ref, logit_grad, g_ref):
    g = lax.dot_general(
        w_ref[0], logit_grad, (((1,), (1,)), ((), ())), preferred_element_type=jnp.float32
    ).astype(g_ref.dtype)
    tok = g_ref.shape[2]
    for z in range(NZH):
        g_ref[z] = g[:, z * tok : (z + 1) * tok]


def first_grads_kernel(s_ref, t_ref, row_ref, w_ref, lg_ref, g_ref):
    @pl.when(pl.program_id(0) == 0)
    def _():
        student_lse, teacher_lse, weight = row_ref[:, 0:1], row_ref[:, 1:2], row_ref[:, 2:3]
        student = jnp.exp(s_ref[...] - student_lse)
        teacher = jnp.exp(t_ref[...].astype(jnp.float32) - teacher_lse)
        lg_ref[...] = (weight * TEMP * (student - teacher)).astype(jnp.bfloat16)

    tile_grads(w_ref, lg_ref[...], g_ref)


def second_grads_kernel(lg_ref, w_ref, g_ref):
    tile_grads(w_ref, lg_ref[...], g_ref)


def over_tiles(kernel, section, ins, weights, whole_outs, grads):
    whole = pl.BlockSpec(memory_space=pltpu.VMEM)
    width = weights.shape[2]
    zs, feats, tok = grads.shape
    return pl.pallas_call(
        kernel,
        grid=(feats // TILE,),
        in_specs=[whole] * len(ins) + [pl.BlockSpec((1, TILE, width), lambda k: (section, k, 0))],
        out_specs=[whole] * len(whole_outs) + [pl.BlockSpec((zs, TILE, tok), lambda k: (0, k, 0))],
        out_shape=[*whole_outs, grads],
        compiler_params=pltpu.CompilerParams(vmem_limit_bytes=16 * 2**20),
        cost_estimate=pl.CostEstimate(
            flops=10**9, bytes_accessed=5 * 10**6, transcendentals=5 * 10**5
        ),
    )(*ins, weights)


def on_device(hidden, head, codes, exponents, loss_weight):
    s = lax.axis_index("section")
    dp = lax.axis_index("dp")
    zh, y = dp // NY, dp % NY
    rows, cols = head.shape
    width = cols // 4
    tok = hidden.shape[0]

    def columns(x, ds, dz):
        at = ((zh ^ dz) * 2 + (s ^ ds)) * width
        return lax.dynamic_slice_in_dim(x, at, width, axis=1)

    def both(mine, other):
        return jnp.where(
            zh == 0, jnp.concatenate([mine, other]), jnp.concatenate([other, mine])
        )

    away = lax.dynamic_slice_in_dim(head, (zh ^ 1) * 2 * width, 2 * width, axis=1)
    first = after(head, away)
    near = jnp.concatenate([columns(first, 0, 0), flip(columns(first, 1, 0), 1, 0)], axis=0)
    near_parts = ring(near)
    came = flip(away, 0, 1)
    came_mine = lax.dynamic_slice_in_dim(
        after(came, near_parts[3][2], near_parts[4][2]), s * width, width, axis=1
    )
    came_send = lax.dynamic_slice_in_dim(came, (s ^ 1) * width, width, axis=1)
    far = jnp.concatenate([came_mine, flip(came_send, 1, 0)], axis=0)
    far_parts = ring(far)

    weights = jnp.zeros((2, NZH, NY, rows, width), head.dtype)
    for dz, parts in enumerate([near_parts, far_parts]):
        for dy, at, block in parts:
            block = block.reshape(-1, 1, 1, rows, width)
            weights = lax.dynamic_update_slice(
                weights, block, (at // rows, zh ^ dz, (y + dy) % NY, 0, 0)
            )
    weights = weights.reshape(2 * NZH * NY * rows, width)

    hidden = after(hidden, near_parts[1][2])
    h_sec = both(hidden, after(flip(hidden, 0, 1), far_parts[3][2], far_parts[4][2]))
    h_all = jnp.concatenate([h_sec, flip(h_sec, 1, 0)], axis=1)
    teacher = teacher_half(codes, exponents)
    t_send = after(columns(teacher, 0, 1), near_parts[3][2])
    scaled_t = both(columns(teacher, 0, 0), flip(t_send, 0, 1))

    logits = jnp.dot(h_all, weights, preferred_element_type=jnp.float32)
    scaled_s = logits / TEMP
    m = jnp.max(scaled_s, axis=1)
    t_wide = scaled_t.astype(jnp.float32)
    t_exp = jnp.exp(t_wide)
    stats = jnp.stack(
        [
            m,
            jnp.sum(jnp.exp(scaled_s - m[:, None]), axis=1),
            jnp.sum(t_exp, axis=1),
            jnp.sum(t_exp * (t_wide - scaled_s), axis=1),
        ]
    ).reshape(8, tok)

    stats = jnp.stack([stats, flip(stats, 1, 0)])
    top = jnp.max(stats[:, 0:2], axis=0)
    s_sum = jnp.sum(stats[:, 2:4] * jnp.exp(stats[:, 0:2] - top), axis=0)
    rest = jnp.sum(stats[:, 4:8], axis=0)
    tiles = [
        jnp.concatenate([top, s_sum, rest[0:2], rest[2 + z : 3 + z], loss_weight[None]])
        for z in range(NZH)
    ]
    parts = jnp.broadcast_to(jnp.stack(tiles)[:, None], (NZH, NQ, 8, tok))
    parts = exchange(parts.reshape(NZH * NQ, 8, tok))
    top = jnp.max(parts[:, 0:2], axis=0)
    s_sum = jnp.sum(parts[:, 2:4] * jnp.exp(parts[:, 0:2] - top), axis=0)
    t_sum = jnp.sum(parts[:, 4:6], axis=0)
    cross = jnp.sum(parts[:, 6], axis=0)
    weight = jnp.concatenate([parts[0, 7], parts[NQ, 7]])
    student_lse = top + jnp.log(s_sum)
    teacher_lse = jnp.log(t_sum)

    def of_mine(a):
        return lax.dynamic_index_in_dim(a, zh, axis=0, keepdims=False)

    kl_loss = cross / of_mine(t_sum) - of_mine(teacher_lse) + of_mine(student_lse)
    kl_loss = TEMP * TEMP * kl_loss

    student_lse, teacher_lse = student_lse.reshape(2 * tok), teacher_lse.reshape(2 * tok)
    per_row = jnp.stack([student_lse, teacher_lse, weight], axis=1)
    w = weights.reshape(2, -1, width)
    feats = w.shape[1]
    logit_grad, g = over_tiles(
        first_grads_kernel,
        1,
        (scaled_s, scaled_t, per_row),
        w,
        [jax.ShapeDtypeStruct(scaled_s.shape, jnp.bfloat16)],
        jax.ShapeDtypeStruct((NZH, feats, tok), jnp.bfloat16),
    )
    theirs = flip(g, 1, 0)
    (mine,) = over_tiles(
        second_grads_kernel,
        0,
        (logit_grad,),
        w,
        [],
        jax.ShapeDtypeStruct((NZH, feats, tok), jnp.float32),
    )
    g = (mine + theirs.astype(jnp.float32)).astype(jnp.bfloat16)
    g = g.reshape(NZH * NQ, rows, tok)
    g = exchange(g)
    g = jnp.sum(g.astype(jnp.float32), axis=0)
    return (kl_loss, g.T.astype(jnp.bfloat16))


def solution(mesh):
    in_specs = (
        P("dp", "section"),
        P(("section", "dp"), "vocab"),
        P("dp", "vocab"),
        P("dp", "vocab"),
        P("dp"),
    )
    out_specs = (P("dp"), P("dp", ("section", "vocab")))
    return jax.shard_map(
        on_device, mesh=mesh, in_specs=in_specs, out_specs=out_specs, check_vma=False
    )
```
